128 devices in a mesh: seq: 32 (over z, x, core), head: 4 (over y).
Axes of the slice: x: 4, y: 4, z: 4, core: 2. Of those that a mesh axis runs over, the one named last changes fastest.
Arguments:
- tokens: bfloat16 [16384, 2048], P('seq'), may hold values from -6 to 6
- cotangent: bfloat16 [16384, 2048], P('seq'), may hold values from -6 to 6
- w_query: bfloat16 [2048, 2048], P(None, 'head'), may hold values from -0.61871843 to 0.61871843
- w_key: bfloat16 [2048, 2048], P(None, 'head'), may hold values from -0.61871843 to 0.61871843
- w_value: bfloat16 [2048, 2048], P(None, 'head'), may hold values from -0.61871843 to 0.61871843
- w_out: bfloat16 [2048, 2048], P('head'), may hold values from -0.61871843 to 0.61871843
- seeds: int32 [4], replicated, may hold values from 0 to 32748
Outputs:
- attended: bfloat16 [16384, 2048], P('seq', 'head')
- grad_tokens: bfloat16 [16384, 2048], P('seq', 'head')
- grad_w_query: float32 [2048, 2048], P('seq', 'head')
- grad_w_key: float32 [2048, 2048], P('seq', 'head')
- grad_w_value: float32 [2048, 2048], P('seq', 'head')
- grad_w_out: float32 [2048, 2048], P('head', 'seq')
The draws below stay inside these ranges and needn't reach their ends.
All inputs are finite; a program needn't handle non-finite values.
Results may differ from the reference program's by a relative error of at most 0.013.
The reference program's roundings to bfloat16 on the way count: a program that leaves them out, or rounds other values in their place, can miss the bound.
Values may be sent and summed in bfloat16 or wider, within the bound.
No kernel may reach another device: no remote copies, remote signals or barrier semaphores. Data moves between devices by JAX's collectives and lax.ppermute only.
A program may use at most 192 MiB of HBM per device.

```python
import math
import jax
import jax.numpy as jnp
from jax import lax

D = 2048
HEADS = 16
DH = 128
LEAF = 128
TOKENS = 16384


def scaled_grid(key, row_total, col_total, low, high):
    key_base = jax.random.fold_in(key, 0)
    key_rows = jax.random.fold_in(key, 2)
    key_cols = jax.random.fold_in(key, 3)
    base_draw = jax.random.truncated_normal(key_base, -4.0, 4.0, (row_total, col_total), jnp.float32)
    blended = base_draw
    row_scale = jnp.exp(jax.random.uniform(key_rows, (row_total, 1), jnp.float32, math.log(low), math.log(high)))
    col_scale = jnp.exp(jax.random.uniform(key_cols, (1, col_total), jnp.float32, math.log(low), math.log(high)))
    return (blended * row_scale * col_scale / math.sqrt(row_total)).astype(jnp.bfloat16)


def draw_w_query(key, part):
    key = jax.random.fold_in(key, 11)
    return scaled_grid(key, D, D, 0.4, 2.5)


def draw_w_key(key, part):
    key = jax.random.fold_in(key, 23)
    return scaled_grid(key, D, D, 0.4, 2.5)


def draw_w_value(key, part):
    key = jax.random.fold_in(key, 37)
    return scaled_grid(key, D, D, 0.4, 2.5)


def draw_w_out(key, part):
    key = jax.random.fold_in(key, 41)
    return scaled_grid(key, D, D, 0.4, 2.5)


def place_ends(values, key, least, high):
    shape = values.shape
    place = [jax.random.randint(jax.random.fold_in(key, axis), (), 0, shape[axis]) for axis in range(len(shape))]
    values = values.at[tuple(place)].set(least)
    longest = shape.index(max(shape))
    place[longest] = (place[longest] + 1) % shape[longest]
    return values.at[tuple(place)].set(high)


def block_scale(rng, shape, cuts, least, high):
    factor_of, own = 1.0, jax.random.fold_in(rng, 6)
    for position, shards_of in cuts:
        draws = jnp.exp(jax.random.uniform(jax.random.fold_in(own, position), (shards_of,), jnp.float32, least / len(cuts), high / len(cuts)))
        factor_of = factor_of * jnp.repeat(draws, shape[position] // shards_of).reshape([-1 if axis == position else 1 for axis in range(len(shape))])
    return factor_of


def centred(key, shape, scale, reach, shards=(), kind=jnp.bfloat16):
    gain = block_scale(key, shape, shards, -0.22, 0.18) if shards else 1.0
    result = jax.random.normal(key, shape, jnp.float32) * scale * gain
    return jnp.minimum(jnp.maximum(result, -reach), reach).astype(kind)


def setup_inputs(seed: int = 0) -> dict:
    arg_keys = jax.random.split(jax.random.key(seed), 8)
    return {
        "tokens": centred(arg_keys[0], (TOKENS, D), 1.0, 6.0, ((0, 32),)),
        "cotangent": centred(arg_keys[1], (TOKENS, D), 1.0, 6.0, ((0, 32),)),
        "w_query": draw_w_query(jax.random.fold_in(arg_keys[7], 71), 0),
        "w_key": draw_w_key(jax.random.fold_in(arg_keys[7], 71), 0),
        "w_value": draw_w_value(jax.random.fold_in(arg_keys[7], 71), 0),
        "w_out": draw_w_out(jax.random.fold_in(arg_keys[7], 71), 0),
        "seeds": place_ends(jax.random.randint(arg_keys[6], (4,), 0, 32749), jax.random.fold_in(arg_keys[6], 1), 0, 32748).astype(jnp.int32),
    }


soft_cap = 6.0
noise_level = 0.5
prime_mod = 32749

def noise_grid(row_ids, col_ids, seed_value):
    row_part = row_ids[:, None]
    col_part = col_ids[None, :]
    hashed = (row_part * 7919 % prime_mod + col_part * 10007 % prime_mod + seed_value * 31337 % prime_mod) % prime_mod
    hashed = (hashed * hashed + col_part) % prime_mod
    hashed = (hashed * hashed + row_part) % prime_mod
    return hashed.astype(jnp.float32) * (2.0 / (prime_mod - 1)) - 1.0

def perturb(weight, noise, axis_no):
    as_float = weight.astype(jnp.float32)
    spread = jnp.sqrt(lax.optimization_barrier(jnp.mean(as_float * as_float, axis=axis_no, keepdims=True)) + 1e-06)
    return (as_float + noise_level * spread * noise).astype(jnp.bfloat16)

def halve_rows(rows_in):
    paired = rows_in.astype(jnp.float32).reshape((rows_in.shape[0] // 2, 2) + rows_in.shape[1:])
    return ((paired[:, 0] + paired[:, 1]) * 0.5).astype(jnp.bfloat16)

def expand_rows(grad_rows):
    return jnp.repeat(grad_rows * 0.5, 2, axis=0)

def flip_pairs(blocks):
    return blocks.reshape((blocks.shape[0] // 2, 2) + blocks.shape[1:])[:, ::-1].reshape(blocks.shape)

def group_view(array_in, groups):
    return array_in.reshape((groups, array_in.shape[0] // groups) + array_in.shape[1:])

def rounded(array_in):
    return lax.optimization_barrier(array_in.astype(jnp.bfloat16)).astype(jnp.float32)

def forward_set(queries, key_rows, value_rows, multiplicity):
    scale_q = 1.0 / math.sqrt(queries.shape[-1])
    scores = jnp.einsum('gqhd,gkhd->gqhk', queries.astype(jnp.float32), key_rows.astype(jnp.float32)) * scale_q
    capped = jnp.tanh(scores / soft_cap)
    weights = multiplicity * jnp.exp(soft_cap * capped)
    numerator = jnp.einsum('gqhk,gkhd->gqhd', rounded(weights), value_rows.astype(jnp.float32))
    return (lax.optimization_barrier(jnp.sum(weights, axis=-1)), numerator)

def backward_set(queries, key_rows, value_rows, grad_out, weight_sum, row_delta, multiplicity):
    scale_q = 1.0 / math.sqrt(queries.shape[-1])
    scores = jnp.einsum('gqhd,gkhd->gqhk', queries.astype(jnp.float32), key_rows.astype(jnp.float32)) * scale_q
    capped = jnp.tanh(scores / soft_cap)
    weights = multiplicity * jnp.exp(soft_cap * capped)
    probability = weights / weight_sum[..., None]
    grad_values = jnp.einsum('gqhk,gqhd->gkhd', rounded(probability), grad_out.astype(jnp.float32))
    grad_prob = jnp.einsum('gqhd,gkhd->gqhk', grad_out.astype(jnp.float32), value_rows.astype(jnp.float32))
    grad_scores = rounded(probability * (grad_prob - row_delta[..., None]) * (1.0 - capped * capped))
    grad_queries = jnp.einsum('gqhk,gkhd->gqhd', grad_scores, key_rows.astype(jnp.float32)) * scale_q
    grad_keys = jnp.einsum('gqhk,gqhd->gkhd', grad_scores, queries.astype(jnp.float32)) * scale_q
    return (grad_queries, grad_keys, grad_values)

def arrange(queries, key_rows, value_rows, flipped):
    groups = key_rows.shape[0] // LEAF
    key_view = group_view(key_rows, groups)
    value_view = group_view(value_rows, groups)
    if flipped:
        key_view = flip_pairs(key_view)
        value_view = flip_pairs(value_view)
    return (group_view(queries, groups), key_view, value_view, groups)

def reference(tokens, cotangent, w_query, w_key, w_value, w_out, seeds):
    all_ids = jnp.arange(D, dtype=jnp.int32)
    query_w = perturb(w_query, noise_grid(all_ids, all_ids, seeds[0]), 0)
    key_w = perturb(w_key, noise_grid(all_ids, all_ids, seeds[1]), 0)
    value_w = perturb(w_value, noise_grid(all_ids, all_ids, seeds[2]), 0)
    out_w = perturb(w_out, noise_grid(all_ids, all_ids, seeds[3]), 1)
    head_shape = (TOKENS, HEADS, DH)
    queries = jnp.dot(tokens, query_w, preferred_element_type=jnp.float32).astype(jnp.bfloat16).reshape(head_shape)
    key_all = jnp.dot(tokens, key_w, preferred_element_type=jnp.float32).astype(jnp.bfloat16).reshape(head_shape)
    value_all = jnp.dot(tokens, value_w, preferred_element_type=jnp.float32).astype(jnp.bfloat16).reshape(head_shape)
    levels = (TOKENS // LEAF).bit_length() - 1
    key_levels = [key_all]
    value_levels = [value_all]
    for level_no in range(1, levels):
        key_levels.append(halve_rows(key_levels[-1]))
        value_levels.append(halve_rows(value_levels[-1]))
    all_sets = [(0, False, 1.0)] + [(level_no, True, 2.0 ** level_no) for level_no in range(levels)]
    weight_sum = jnp.zeros((TOKENS, HEADS), jnp.float32)
    numerator = jnp.zeros(head_shape, jnp.float32)
    for level_no, flipped, multiplicity in all_sets:
        query_view, key_view, value_view, groups = arrange(queries, key_levels[level_no], value_levels[level_no], flipped)
        part_sum, part_num = forward_set(query_view, key_view, value_view, multiplicity)
        weight_sum = weight_sum + part_sum.reshape(TOKENS, HEADS)
        numerator = numerator + part_num.reshape(head_shape)
    attention = (numerator / weight_sum[..., None]).astype(jnp.bfloat16)
    flat_attention = attention.reshape(TOKENS, D)
    attended = jnp.dot(flat_attention, out_w, preferred_element_type=jnp.float32).astype(jnp.bfloat16)
    grad_attention = jnp.dot(cotangent, out_w.T, preferred_element_type=jnp.float32).astype(jnp.bfloat16)
    grad_heads = grad_attention.reshape(head_shape)
    row_delta = lax.optimization_barrier(jnp.sum(grad_heads.astype(jnp.float32) * attention.astype(jnp.float32), axis=-1))
    grad_q = jnp.zeros(head_shape, jnp.float32)
    key_grads = [jnp.zeros(k_rows.shape, jnp.float32) for k_rows in key_levels]
    value_grads = [jnp.zeros(v_rows.shape, jnp.float32) for v_rows in value_levels]
    for level_no, flipped, multiplicity in all_sets:
        query_view, key_view, value_view, groups = arrange(queries, key_levels[level_no], value_levels[level_no], flipped)
        dq_part, dk_part, dv_part = backward_set(query_view, key_view, value_view, group_view(grad_heads, groups), group_view(weight_sum, groups), group_view(row_delta, groups), multiplicity)
        grad_q = grad_q + dq_part.reshape(head_shape)
        if flipped:
            dk_part = flip_pairs(dk_part)
            dv_part = flip_pairs(dv_part)
        key_grads[level_no] = key_grads[level_no] + dk_part.reshape(key_levels[level_no].shape)
        value_grads[level_no] = value_grads[level_no] + dv_part.reshape(value_levels[level_no].shape)
    upper_k = key_grads[-1]
    upper_v = value_grads[-1]
    for level_no in reversed(range(levels - 1)):
        upper_k = key_grads[level_no] + expand_rows(upper_k)
        upper_v = value_grads[level_no] + expand_rows(upper_v)
    dq_flat = grad_q.astype(jnp.bfloat16).reshape(TOKENS, D)
    dk_flat = upper_k.astype(jnp.bfloat16).reshape(TOKENS, D)
    dv_flat = upper_v.astype(jnp.bfloat16).reshape(TOKENS, D)
    grads_cat = jnp.concatenate([dq_flat, dk_flat, dv_flat], axis=1)
    weights_cat = jnp.concatenate([query_w, key_w, value_w], axis=1)
    grad_tokens = jnp.dot(grads_cat, weights_cat.T, preferred_element_type=jnp.float32).astype(jnp.bfloat16)
    grad_w_query = jnp.dot(tokens.T, dq_flat, preferred_element_type=jnp.float32)
    grad_w_key = jnp.dot(tokens.T, dk_flat, preferred_element_type=jnp.float32)
    grad_w_value = jnp.dot(tokens.T, dv_flat, preferred_element_type=jnp.float32)
    grad_w_out = jnp.dot(flat_attention.T, cotangent, preferred_element_type=jnp.float32)
    return (attended, grad_tokens, grad_w_query, grad_w_key, grad_w_value, grad_w_out)
```

```python
import functools
import math

import jax
import jax.numpy as jnp
from jax import lax
from jax.experimental import pallas as pl
from jax.experimental.pallas import tpu as pltpu
from jax.sharding import Mesh, PartitionSpec as P

DH = 128
LEAF = 128
PRIME = 32749
CAP = 6.0
HALF_NOISE = 0.5
SCALE = 1.0 / math.sqrt(DH)
BF = jnp.bfloat16
F32 = jnp.float32
SEQ = ("z", "x", "core")
VMEM = pl.BlockSpec(memory_space=pltpu.VMEM)
SMEM = pl.BlockSpec(memory_space=pltpu.SMEM)


def call(kernel, outs, args, flops, name, scratch=(), specs=None):
    bytes_moved = sum(a.size * a.dtype.itemsize for a in (*args, *outs))
    return pl.pallas_call(
        kernel,
        out_shape=list(outs),
        in_specs=specs or [VMEM] * len(args),
        out_specs=[VMEM] * len(outs),
        scratch_shapes=list(scratch),
        name=name,
        cost_estimate=pl.CostEstimate(flops=flops, bytes_accessed=bytes_moved, transcendentals=0),
        compiler_params=pltpu.CompilerParams(vmem_limit_bytes=48 << 20),
    )(*args)


def shape(rows, cols, dtype):
    return jax.ShapeDtypeStruct((rows, cols), dtype)


def dot(a, b):
    return jnp.dot(a, b, preferred_element_type=F32)


def dot_bt(a, b):
    return lax.dot_general(a, b, (((1,), (1,)), ((), ())), preferred_element_type=F32)


def dot_at(a, b):
    return lax.dot_general(a, b, (((0,), (0,)), ((), ())), preferred_element_type=F32)


def halver(rows):
    out_row = lax.broadcasted_iota(jnp.int32, (rows // 2, rows), 0)
    in_row = lax.broadcasted_iota(jnp.int32, (rows // 2, rows), 1)
    return jnp.where(lax.shift_right_logical(in_row, 1) == out_row, 0.5, 0.0).astype(BF)


def halve(rows_in):
    return dot(halver(rows_in.shape[0]), rows_in).astype(BF)


def expand(rows_in, shift=1):
    rows, times = rows_in.shape[0], 1 << shift
    out_row = lax.broadcasted_iota(jnp.int32, (rows * times, rows), 0)
    in_row = lax.broadcasted_iota(jnp.int32, (rows * times, rows), 1)
    spread = jnp.where(lax.shift_right_logical(out_row, shift) == in_row, 1.0 / times, 0.0).astype(BF)
    high = rows_in.astype(BF)
    low = (rows_in - high.astype(F32)).astype(BF)
    return dot(spread, high) + dot(spread, low)


def fold(value):
    for _ in range(2):
        value = lax.shift_right_logical(value, 15) * 19 + (value & 32767)
    return value


def below_prime(value):
    return jnp.where(value >= PRIME, value - PRIME, value)


def hashed_noise(row_part, col_part, row_ids, col_ids):
    h = below_prime(row_part + col_part)
    h = fold(h * h + col_ids)
    h = below_prime(fold(h * h + row_ids))
    return h.astype(F32) * (2.0 / (PRIME - 1)) - 1.0


def column_noise_kernel(col_ids_ref, col_part_ref, *refs):
    w_refs, out_ref = refs[:-1], refs[-1]
    rows, cols = w_refs[0].shape
    chunk = 64
    lanes = cols // 128
    amps = []
    for w_ref in w_refs:

        def add_squares(i, acc, w_ref=w_ref):
            w = w_ref[pl.ds(pl.multiple_of(i * 128, 128), 128), :].astype(F32)
            return acc + jnp.sum((w * w).reshape(16, 8, cols), axis=0)

        acc = lax.fori_loop(0, rows // 128, add_squares, jnp.zeros((8, cols), F32))
        mean = jnp.sum(acc, axis=0, keepdims=True) * (1.0 / rows)
        amps.append(HALF_NOISE * jnp.sqrt(mean + 1e-06))

    def step(i, _):
        base = pl.multiple_of(i * chunk, chunk)
        row_ids = lax.broadcasted_iota(jnp.int32, (chunk, 128), 0) + base
        row_part = below_prime(fold(row_ids * 7919))
        for n, w_ref in enumerate(w_refs):
            for lane in range(lanes):
                here = slice(lane * 128, lane * 128 + 128)
                there = slice(n * cols + lane * 128, n * cols + lane * 128 + 128)
                noise = hashed_noise(row_part, col_part_ref[:, there], row_ids, col_ids_ref[:, there])
                w = w_ref[pl.ds(base, chunk), here].astype(F32)
                out_ref[pl.ds(base, chunk), there] = (w + amps[n][:, here] * noise).astype(BF)
        return 0

    lax.fori_loop(0, rows // chunk, step, 0)


def row_noise_kernel(base_ref, col_part_ref, w_ref, out_ref):
    rows, cols = w_ref.shape
    chunk = 32

    def step(i, _):
        start = pl.multiple_of(i * chunk, chunk)
        row_ids = lax.broadcasted_iota(jnp.int32, (chunk, 128), 0) + start + base_ref[0]
        row_part = below_prime(fold(row_ids * 7919))
        col_ids = lax.broadcasted_iota(jnp.int32, (1, 128), 1)
        acc = jnp.zeros((chunk, 128), F32)
        for lane in range(cols // 128):
            w = w_ref[pl.ds(start, chunk), lane * 128 : lane * 128 + 128].astype(F32)
            acc = acc + w * w
        mean = jnp.sum(acc, axis=1, keepdims=True) * (1.0 / cols)
        amp = jnp.broadcast_to(HALF_NOISE * jnp.sqrt(mean + 1e-06), (chunk, 128))
        for lane in range(cols // 128):
            here = slice(lane * 128, lane * 128 + 128)
            noise = hashed_noise(row_part, col_part_ref[:, here], row_ids, col_ids + lane * 128)
            w = w_ref[pl.ds(start, chunk), here].astype(F32)
            out_ref[pl.ds(start, chunk), here] = (w + amp * noise).astype(BF)
        return 0

    lax.fori_loop(0, rows // chunk, step, 0)


def perturb_columns(weights, own_ids, seeds):
    ids = jnp.tile(own_ids, len(weights))[None]
    parts = [(own_ids * 10007 % PRIME + seed * 31337 % PRIME) % PRIME for seed in seeds]
    rows, cols = weights[0].shape
    return call(
        column_noise_kernel,
        [shape(rows, cols * len(weights), BF)],
        [ids, jnp.concatenate(parts)[None], *weights],
        60 * 200 * rows * cols * len(weights) // 100,
        "perturb_columns",
    )[0]


def perturb_rows(weight, base, all_ids, seed):
    part = ((all_ids * 10007 % PRIME + seed * 31337 % PRIME) % PRIME)[None]
    return call(
        row_noise_kernel,
        [shape(*weight.shape, BF)],
        [base.reshape(1), part, weight],
        120 * weight.size,
        "perturb_rows",
        specs=[SMEM, VMEM, VMEM],
    )[0]


def head_cols(h):
    return pl.ds(pl.multiple_of(h * DH, DH), DH)


def scores(q, k, mult):
    t = jnp.tanh(dot_bt(q, k) * (SCALE / CAP))
    w = jnp.exp(CAP * t)
    return t, (w if mult is None else w * mult)


def gather_local(kv_ref, kv1_ref, kl_ref, vl_ref):
    width = kl_ref.shape[2]
    for pair in range(2):
        for into, off in ((kl_ref, 0), (vl_ref, width)):
            into[pair, :256, :] = kv_ref[pair * 256 : pair * 256 + 256, off : off + width]
            into[pair, 256:, :] = kv1_ref[(1 - pair) * 128 : (1 - pair) * 128 + 128, off : off + width]


def local_mult():
    lane = lax.broadcasted_iota(jnp.int32, (1, 384), 1)
    return jnp.where(lane < 256, 1.0, 2.0)


def levels_kernel(kv_ref, kv1_ref, kv2_ref):
    kv1_ref[...] = halve(kv_ref[...])
    kv2_ref[...] = halve(kv1_ref[...])


def local_forward_kernel(q_ref, kv_ref, kv1_ref, num_ref, sum_ref, kl_ref, vl_ref):
    gather_local(kv_ref, kv1_ref, kl_ref, vl_ref)
    mult = local_mult()

    def head(h, _):
        hs = head_cols(h)
        for pair in range(2):
            rows = slice(pair * 256, pair * 256 + 256)
            _, w = scores(q_ref[rows, hs], kl_ref[pair, :, hs], mult)
            num_ref[rows, hs] = dot(w.astype(BF), vl_ref[pair, :, hs])
            sum_ref[rows, hs] = jnp.broadcast_to(jnp.sum(w, axis=1, keepdims=True), (256, DH))
        return 0

    lax.fori_loop(0, q_ref.shape[1] // DH, head, 0)


def far_kernel(place_ref, q_ref, kv2_ref, mine_a, mine_b, their_a, their_b, num_ref, sum_ref, ga_ref,
               att_ref, inv_ref, rd_ref, dq_ref, keep_ref, send_ref, kf, vf, dkf, dvf):
    core = place_ref[0]
    z_odd = place_ref[2] & 1
    width = q_ref.shape[1]
    kf[:128, :] = kv2_ref[:, :width]
    vf[:128, :] = kv2_ref[:, width:]
    for is_core, (into_mine, into_their) in ((0, (kf, vf)), (1, (vf, kf))):

        @pl.when(core == is_core)
        def _():
            for into, first, second in ((into_mine, mine_a, mine_b), (into_their, their_a, their_b)):
                into[128:384, :] = first[...]
                into[384:512, :] = second[:128, :]
                into[pl.ds(pl.multiple_of(512 + 64 * z_odd, 64), 64), :] = second[128:192, :]
                into[pl.ds(pl.multiple_of(576 - 64 * z_odd, 64), 64), :] = second[192:, :]

    lane = lax.broadcasted_iota(jnp.int32, (1, 640), 1)
    mult = lax.shift_left(jnp.int32(4), lax.shift_right_logical(lane, 7)).astype(F32)

    def head(h, _):
        hs = head_cols(h)
        q, k, v, ga = q_ref[:, hs], kf[:, hs], vf[:, hs], ga_ref[:, hs]
        t, w = scores(q, k, mult)
        total = sum_ref[:, hs][:, :1] + jnp.sum(w, axis=1, keepdims=True)
        inv = 1.0 / total
        att = ((num_ref[:, hs] + dot(w.astype(BF), v)) * inv).astype(BF)
        att_ref[:, hs] = att
        rd = jnp.sum(ga.astype(F32) * att.astype(F32), axis=1, keepdims=True)
        inv_ref[:, hs] = jnp.broadcast_to(inv, (inv.shape[0], DH))
        rd_ref[:, hs] = jnp.broadcast_to(rd, (rd.shape[0], DH))
        p = w * inv
        dvf[:, hs] = dot_at(p.astype(BF), ga)
        g = (p * (dot_bt(ga, v) - rd) * (1.0 - t * t)).astype(BF)
        dq_ref[:, hs] = dot(g, k) * SCALE
        dkf[:, hs] = dot_at(g, q) * SCALE
        return 0

    lax.fori_loop(0, width // DH, head, 0)
    send_ref[:128, :] = dkf[:128, :].astype(BF)
    send_ref[128:256, :] = dvf[:128, :].astype(BF)
    for is_core, (keep, give) in ((0, (dkf, dvf)), (1, (dvf, dkf))):

        @pl.when(core == is_core)
        def _():
            keep_ref[...] = keep[128:, :]
            send_ref[256:, :] = give[128:, :].astype(BF)


def local_backward_kernel(q_ref, kv_ref, kv1_ref, inv_ref, rd_ref, ga_ref, dqf_ref,
                          dq_ref, dkv_ref, kl_ref, vl_ref, d1_ref):
    gather_local(kv_ref, kv1_ref, kl_ref, vl_ref)
    mult = local_mult()
    width = q_ref.shape[1]

    def head(h, _):
        hs = head_cols(h)
        hv = pl.ds(pl.multiple_of(width + h * DH, DH), DH)
        for pair in range(2):
            rows = slice(pair * 256, pair * 256 + 256)
            other = slice((1 - pair) * 128, (1 - pair) * 128 + 128)
            q, ga, k, v = q_ref[rows, hs], ga_ref[rows, hs], kl_ref[pair, :, hs], vl_ref[pair, :, hs]
            t, w = scores(q, k, mult)
            p = w * inv_ref[rows, hs][:, :1]
            dv = dot_at(p.astype(BF), ga)
            g = (p * (dot_bt(ga, v) - rd_ref[rows, hs][:, :1]) * (1.0 - t * t)).astype(BF)
            dq_ref[rows, hs] = (dqf_ref[rows, hs] + dot(g, k) * SCALE).astype(BF)
            dk = dot_at(g, q) * SCALE
            dkv_ref[rows, hs] = dk[:256]
            dkv_ref[rows, hv] = dv[:256]
            d1_ref[other, hs] = dk[256:]
            d1_ref[other, hv] = dv[256:]
        return 0

    lax.fori_loop(0, width // DH, head, 0)
    dkv_ref[...] += expand(d1_ref[...])


def out_core_kernel(place_ref, own_ref, other_ref, chip_ref, chip_next_ref):
    core = place_ref[0]
    width = chip_ref.shape[1]
    for is_core in range(2):

        @pl.when(core == is_core)
        def _():
            cols = slice(is_core * width, is_core * width + width)
            chip_ref[is_core * 64 : is_core * 64 + 64, :] = halve(own_ref[:, cols])
            chip_ref[64 - is_core * 64 : 128 - is_core * 64, :] = halve(other_ref[:, cols])

    chip_next_ref[...] = halve(chip_ref[...])


def out_x_kernel(place_ref, own_ref, one_ref, two_ref, three_ref, sets_ref, row_ref, row_next_ref):
    x = place_ref[1]
    odd = x & 1
    sets_ref[:128, :] = one_ref[...]
    sets_ref[pl.ds(pl.multiple_of(128 + 64 * odd, 64), 64), :] = two_ref[...]
    sets_ref[pl.ds(pl.multiple_of(192 - 64 * odd, 64), 64), :] = three_ref[...]
    for apart, part in ((0, own_ref[...]), (1, halve(one_ref[...])), (2, two_ref[...]), (3, three_ref[...])):
        row_ref[pl.ds(pl.multiple_of(32 * (x ^ apart), 32), 32), :] = halve(part)
    row_next_ref[...] = halve(row_ref[...])


def back_core_kernel(place_ref, keep_ref, got_ref, near_ref, one_ref, two_ref, three_ref):
    odd = place_ref[2] & 1
    near_ref[...] = keep_ref[:256, :] + got_ref[256:512, :].astype(F32)
    one_ref[...] = (keep_ref[256:384, :] + got_ref[512:640, :].astype(F32)).astype(BF)
    for into, first in ((two_ref, odd), (three_ref, 1 - odd)):
        kept = keep_ref[pl.ds(pl.multiple_of(384 + 64 * first, 64), 64), :]
        got = got_ref[pl.ds(pl.multiple_of(640 + 64 * first, 64), 64), :].astype(F32)
        into[...] = (kept + got).astype(BF)


def back_z_kernel(place_ref, near_ref, one_ref, two_ref, three_ref, own_out, one_out, two_out, three_out, row_ref):
    x = place_ref[1]
    odd = x & 1
    row_ref[...] = one_ref[...].astype(F32) + expand(two_ref[...].astype(F32) + three_ref[...].astype(F32))

    def part(apart):
        return row_ref[pl.ds(pl.multiple_of(32 * (x ^ apart), 32), 32), :]

    own_out[...] = part(0)
    one_out[...] = (near_ref[:128, :] + expand(part(1), 2)).astype(BF)
    for into, apart, first in ((two_out, 2, odd), (three_out, 3, 1 - odd)):
        near = near_ref[pl.ds(pl.multiple_of(128 + 64 * first, 64), 64), :]
        into[...] = (near + expand(part(apart))).astype(BF)


def back_x_kernel(place_ref, own_ref, one_ref, two_ref, three_ref, keep_ref, send_ref, chip_ref):
    core = place_ref[0]
    pair = two_ref[...].astype(F32) + three_ref[...].astype(F32) + expand(own_ref[...])
    chip_ref[...] = one_ref[...].astype(F32) + expand(pair)
    keep_ref[...] = chip_ref[pl.ds(pl.multiple_of(64 * core, 64), 64), :]
    send_ref[...] = chip_ref[pl.ds(pl.multiple_of(64 - 64 * core, 64), 64), :].astype(BF)


def back_last_kernel(place_ref, keep_ref, got_ref, got0_ref, dkv_ref, out_ref):
    core = place_ref[0]
    width = keep_ref.shape[1]
    for is_core in range(2):

        @pl.when(core == is_core)
        def _():
            for n in range(2):
                cols = slice(n * width, n * width + width)
                upper = keep_ref[...] if n == is_core else got_ref[...].astype(F32)
                level = got0_ref[n * 128 : n * 128 + 128, :].astype(F32) + expand(upper)
                out_ref[:, cols] = (dkv_ref[:, cols] + expand(level, 2)).astype(BF)


def split_kernel(place_ref, in_ref, mine_ref, other_ref):
    core = place_ref[0]
    for n in range(in_ref.shape[1] // 256):
        a = in_ref[:, n * 256 : n * 256 + 128]
        b = in_ref[:, n * 256 + 128 : n * 256 + 256]
        low = jnp.concatenate([a[:, :64], b[:, :64]], axis=1)
        high = jnp.concatenate([a[:, 64:], b[:, 64:]], axis=1)
        here = slice(n * 128, n * 128 + 128)

        @pl.when(core == 0)
        def _():
            mine_ref[:, here] = low
            other_ref[:, here] = high

        @pl.when(core == 1)
        def _():
            mine_ref[:, here] = high
            other_ref[:, here] = low


def swap(rows, axis, apart):
    return lax.ppermute(rows, axis, [(i, i ^ apart) for i in range(lax.axis_size(axis))])


def shift(rows, axis, by):
    n = lax.axis_size(axis)
    return lax.ppermute(rows, axis, [(i, (i + by) % n) for i in range(n)])


def sum_heads(terms, rank):
    rows, cols = terms.shape[0], terms.shape[1] // 4
    half = rows // 2

    def part(by, first, count):
        return lax.dynamic_slice(terms, (first, (rank + by) % 4 * cols), (count, cols))

    up = shift(part(2, 0, half), "head", 1)
    down = shift(part(2, half, half), "head", -1)
    first = (part(1, 0, half).astype(F32) + up.astype(F32)).astype(BF)
    second = (part(3, half, half).astype(F32) + down.astype(F32)).astype(BF)
    from_below = shift(jnp.concatenate([first, part(1, half, half)], axis=0), "head", 1)
    from_above = shift(jnp.concatenate([part(3, 0, half), second], axis=0), "head", -1)
    own = part(0, 0, rows).astype(F32)
    return (own + from_below.astype(F32) + from_above.astype(F32)).astype(BF)


def sum_chips(terms):
    rows, cols = terms.shape
    parts = lax.all_to_all(terms.reshape(16, rows // 16, cols), ("z", "x"), 0, 0)
    return jnp.sum(parts.astype(F32), axis=0)


def body(tokens, cotangent, w_query, w_key, w_value, w_out, seeds):
    place = jnp.stack([lax.axis_index("core"), lax.axis_index("x"), lax.axis_index("z")]).astype(jnp.int32)
    rank = lax.axis_index("head")
    rows, model = tokens.shape
    width = w_query.shape[1]
    all_ids = jnp.arange(model, dtype=jnp.int32)
    base = (rank * width).astype(jnp.int32)
    own_ids = base + jnp.arange(width, dtype=jnp.int32)
    pair_flops = 2 * rows * DH * width

    kv_w = perturb_columns([w_key, w_value], own_ids, [seeds[1], seeds[2]])
    kv = dot(tokens, kv_w).astype(BF)
    kv1, kv2 = call(levels_kernel, [shape(256, 2 * width, BF), shape(128, 2 * width, BF)], [kv], 1 << 29, "levels")
    kv2_other = swap(kv2, "core", 1)
    place_specs = lambda n: [SMEM] + [VMEM] * n
    chip, chip_next = call(out_core_kernel, [shape(128, width, BF), shape(64, width, BF)],
                           [place, kv2, kv2_other], 1 << 28, "out_core", specs=place_specs(2))
    x1, x2, x3 = swap(chip, "x", 1), swap(chip_next, "x", 2), swap(chip_next, "x", 3)
    mine_a, row, row_next = call(out_x_kernel, [shape(256, width, BF), shape(128, width, BF), shape(64, width, BF)],
                                 [place, chip_next, x1, x2, x3], 1 << 28, "out_x", specs=place_specs(4))
    z1, z2, z3 = swap(row, "z", 1), swap(row_next, "z", 2), swap(row_next, "z", 3)
    mine_b = jnp.concatenate([z1, z2, z3], axis=0)
    their_a = swap(mine_a, "core", 1)
    their_b = swap(mine_b, "core", 1)

    q_w = perturb_columns([w_query], own_ids, [seeds[0]])
    out_w = perturb_rows(w_out, base, all_ids, seeds[3])
    queries = dot(tokens, q_w).astype(BF)
    grad_att = dot_bt(cotangent, out_w).astype(BF)
    tok_mine, tok_give = call(split_kernel, [shape(rows, model // 2, BF)] * 2, [place, tokens], 1 << 28,
                              "split", specs=place_specs(1))
    cot_mine, cot_give = call(split_kernel, [shape(rows, model // 2, BF)] * 2, [place, cotangent], 1 << 28,
                              "split", specs=place_specs(1))
    tok_other = swap(tok_give, "core", 1)
    cot_other = swap(cot_give, "core", 1)
    local_kv = [pltpu.VMEM((2, 384, width), BF)] * 2
    num, total = call(local_forward_kernel, [shape(rows, width, F32)] * 2, [queries, kv, kv1],
                      4 * pair_flops, "local_forward", scratch=local_kv)

    att, inv, rd, dq_far, keep, send = call(
        far_kernel,
        [shape(rows, width, BF)] + [shape(rows, width, F32)] * 3 + [shape(512, width, F32), shape(768, width, BF)],
        [place, queries, kv2_other, mine_a, mine_b, their_a, their_b, num, total, grad_att],
        35 * pair_flops, "far",
        scratch=[pltpu.VMEM((640, width), BF)] * 2 + [pltpu.VMEM((640, width), F32)] * 2,
        specs=place_specs(9),
    )
    got = swap(send, "core", 1)
    att_other = swap(att, "core", 1)

    def weight_grad(lhs, lhs_other, rhs, rhs_other):
        return (dot_at(lhs, rhs) + dot_at(lhs_other, rhs_other)).astype(BF)

    grad_w_out = sum_chips(weight_grad(cot_mine, cot_other, att, att_other))
    attended = sum_heads(dot(att, out_w).astype(BF), rank)

    near, b1, b2, b3 = call(
        back_core_kernel, [shape(256, width, F32), shape(128, width, BF), shape(64, width, BF), shape(64, width, BF)],
        [place, keep, got], 1 << 27, "back_core", specs=place_specs(2))
    b1, b2, b3 = swap(b1, "z", 1), swap(b2, "z", 2), swap(b3, "z", 3)
    own, c1, c2, c3 = call(
        back_z_kernel, [shape(32, width, F32), shape(128, width, BF), shape(64, width, BF), shape(64, width, BF)],
        [place, near, b1, b2, b3], 1 << 28, "back_z", scratch=[pltpu.VMEM((128, width), F32)], specs=place_specs(4))
    c1, c2, c3 = swap(c1, "x", 1), swap(c2, "x", 2), swap(c3, "x", 3)
    keep3, send3 = call(
        back_x_kernel, [shape(64, width, F32), shape(64, width, BF)], [place, own, c1, c2, c3], 1 << 28,
        "back_x", scratch=[pltpu.VMEM((128, width), F32)], specs=place_specs(4))
    got3 = swap(send3, "core", 1)

    dq, dkv_local = call(
        local_backward_kernel, [shape(rows, width, BF), shape(rows, 2 * width, F32)],
        [queries, kv, kv1, inv, rd, grad_att, dq_far], 14 * pair_flops, "local_backward",
        scratch=local_kv + [pltpu.VMEM((256, 2 * width), F32)])
    dq_other = swap(dq, "core", 1)
    grad_w_query = sum_chips(weight_grad(tok_mine, tok_other, dq, dq_other))
    input_terms = dot_bt(dq, q_w)

    dkv = call(back_last_kernel, [shape(rows, 2 * width, BF)], [place, keep3, got3, got[:256], dkv_local],
               1 << 29, "back_last", specs=place_specs(4))[0]
    dkv_other = swap(dkv, "core", 1)
    grad_w_kv = sum_chips(weight_grad(tok_mine, tok_other, dkv, dkv_other))
    input_terms = (input_terms + dot_bt(dkv, kv_w)).astype(BF)
    grad_tokens = sum_heads(input_terms, rank)
    return (attended, grad_tokens, grad_w_query, grad_w_kv[:, :width], grad_w_kv[:, width:], grad_w_out.T)


def solution(mesh):
    fine = Mesh(mesh.devices.reshape(4, 4, 2, 4), SEQ + ("head",))
    in_specs = (
        P(SEQ, None),
        P(SEQ, None),
        P(None, "head"),
        P(None, "head"),
        P(None, "head"),
        P("head", None),
        P(),
    )
    out_specs = (P(SEQ, "head"),) * 5 + (P("head", SEQ),)
    return jax.shard_map(body, mesh=fine, in_specs=in_specs, out_specs=out_specs, check_vma=False)
```

```python
import math

import jax
import jax.numpy as jnp
from jax import lax
from jax.experimental import pallas as pl
from jax.experimental.pallas import tpu as pltpu
from jax.sharding import Mesh, PartitionSpec as P

DH = 128
LEAF = 128
PRIME = 32749
CAP = 6.0
HALF_NOISE = 0.5
SCALE = 1.0 / math.sqrt(DH)
BF = jnp.bfloat16
F32 = jnp.float32
SEQ = ("z", "x", "core")
VMEM = pl.BlockSpec(memory_space=pltpu.VMEM)
SMEM = pl.BlockSpec(memory_space=pltpu.SMEM)
HBM = pl.BlockSpec(memory_space=pltpu.HBM)


def params(mib=24):
    return pltpu.CompilerParams(vmem_limit_bytes=mib << 20)


def time_cost(us):
    return pl.CostEstimate(flops=int(us * 1e9), bytes_accessed=1, transcendentals=0)


class Chain:
    def __init__(self, place):
        self.place, self.tick = place, jnp.zeros((1, 128), F32)

    def __call__(self, kernel, outs, args, scratch=(), us=1.0):
        used = 1 + len(args)

        def run(*refs):
            refs[used + 1][...] = refs[used][...]
            kernel(*refs[:used], *refs[used + 2 :])

        self.tick, *results = pl.pallas_call(
            run,
            out_shape=[shape(1, 128, F32), *outs],
            in_specs=[SMEM] + [VMEM] * (len(args) + 1),
            out_specs=[VMEM] * (len(outs) + 1),
            scratch_shapes=list(scratch),
            name=kernel.__name__,
            cost_estimate=time_cost(us),
            compiler_params=params(),
        )(self.place, *args, self.tick)
        return results


def shape(rows, cols, dtype):
    return jax.ShapeDtypeStruct((rows, cols), dtype)


def dot(a, b):
    return jnp.dot(a, b, preferred_element_type=F32)


def dot_bt(a, b):
    return lax.dot_general(a, b, (((1,), (1,)), ((), ())), preferred_element_type=F32)


def dot_at(a, b):
    return lax.dot_general(a, b, (((0,), (0,)), ((), ())), preferred_element_type=F32)


def rows_at(start, count):
    return pl.ds(pl.multiple_of(start, count), count)


def halve(rows_in):
    rows = rows_in.shape[0]
    out_row = lax.broadcasted_iota(jnp.int32, (rows // 2, rows), 0)
    in_row = lax.broadcasted_iota(jnp.int32, (rows // 2, rows), 1)
    average = jnp.where(lax.shift_right_logical(in_row, 1) == out_row, 0.5, 0.0).astype(BF)
    return dot(average, rows_in).astype(BF)


def expand(rows_in, shift=1):
    rows, times = rows_in.shape[0], 1 << shift
    out_row = lax.broadcasted_iota(jnp.int32, (rows * times, rows), 0)
    in_row = lax.broadcasted_iota(jnp.int32, (rows * times, rows), 1)
    spread = jnp.where(lax.shift_right_logical(out_row, shift) == in_row, 1.0 / times, 0.0).astype(BF)
    high = rows_in.astype(BF)
    low = (rows_in - high.astype(F32)).astype(BF)
    return dot(spread, high) + dot(spread, low)


def fold(value):
    for _ in range(2):
        value = lax.shift_right_logical(value, 15) * 19 + (value & 32767)
    return value


def below_prime(value):
    return jnp.where(value >= PRIME, value - PRIME, value)


def hash_of(row_part, col_part, row_ids, col_ids):
    h = row_part + col_part
    f = h.astype(F32)
    quotient = (f * (f * (1.0 / PRIME))).astype(jnp.int32)
    h = h * h - quotient * PRIME + col_ids
    return below_prime(fold(h * h + row_ids)).astype(F32)


def noise_all(w_ref, out_ref, lane_ids_ref, lane_part_ref, lanes_are_rows):
    rows, cols = w_ref.shape
    chunk, mult = 64, (10007 if lanes_are_rows else 7919)

    def add_squares(i, acc):
        w = w_ref[rows_at(i * 64, 64), :].astype(F32)
        return acc + jnp.sum((w * w).reshape(8, 8, cols), axis=0)

    acc = lax.fori_loop(0, rows // 64, add_squares, jnp.zeros((8, cols), F32))
    mean = jnp.sum(acc, axis=0, keepdims=True) * (1.0 / rows)
    amp = HALF_NOISE * jnp.sqrt(mean + 1e-06)
    slope = amp * (2.0 / (PRIME - 1))

    def step(i, carry):
        ids, part = carry
        for lane in range(cols // 128):
            here = slice(lane * 128, lane * 128 + 128)
            lane_ids, lane_part = lane_ids_ref[:, here], lane_part_ref[:, here]
            if lanes_are_rows:
                hashed = hash_of(lane_part, part, lane_ids, ids)
            else:
                hashed = hash_of(part, lane_part, ids, lane_ids)
            w = w_ref[rows_at(i * chunk, chunk), here].astype(F32)
            out_ref[rows_at(i * chunk, chunk), here] = ((w - amp[:, here]) + slope[:, here] * hashed).astype(BF)
        return ids + chunk, below_prime(part + chunk * mult % PRIME)

    ids = lax.broadcasted_iota(jnp.int32, (chunk, 128), 0)
    lax.fori_loop(0, rows // chunk, step, (ids, ids * mult % PRIME))


def fetch(from_ref, into_ref, sem):
    copy = pltpu.make_async_copy(from_ref, into_ref, sem)
    copy.start()
    copy.wait()


def perturb_same(place_ref, ids_ref, part_ref, w0_ref, w1_ref, tick_in, tick_out, out_ref, w_ref, sem):
    tick_out[...] = tick_in[...]
    for core, from_ref in ((0, w0_ref), (1, w1_ref)):

        @pl.when(place_ref[0] == core)
        def _(from_ref=from_ref):
            fetch(from_ref, w_ref, sem)

    noise_all(w_ref, out_ref, ids_ref, part_ref, False)


def perturb_mixed(place_ref, ids_ref, part_ref, w0_ref, w1_ref, tick_in, tick_out, out_ref, w_ref, sem, wide_ref):
    tick_out[...] = tick_in[...]

    @pl.when(place_ref[0] == 0)
    def _():
        fetch(w0_ref, w_ref, sem)
        noise_all(w_ref, out_ref, ids_ref, part_ref, False)

    @pl.when(place_ref[0] == 1)
    def _():
        fetch(w1_ref, wide_ref, sem)
        for n in range(w_ref.shape[0] // 128):
            w_ref[n * 128 : n * 128 + 128, :] = wide_ref[:, n * 128 : n * 128 + 128].T
        noise_all(w_ref, out_ref, ids_ref, part_ref, True)


def perturb(kernel, run, core, rank, w0, w1, seed0, seed1, mult1, mib):
    rows, cols = w0.shape
    ids = rank * cols + jnp.arange(cols, dtype=jnp.int32)
    mult, seed = jnp.where(core == 0, 10007, mult1), jnp.where(core == 0, seed0, seed1)
    part = (ids * mult % PRIME + seed * 31337 % PRIME) % PRIME
    wide = [pltpu.VMEM(w1.shape, BF)] if w1.shape != w0.shape else []
    run.tick, out = pl.pallas_call(
        kernel,
        out_shape=[shape(1, 128, F32), shape(rows, cols, BF)],
        in_specs=[SMEM, VMEM, VMEM, HBM, HBM, VMEM],
        out_specs=[VMEM, VMEM],
        scratch_shapes=[pltpu.VMEM((rows, cols), BF), pltpu.SemaphoreType.DMA] + wide,
        name=kernel.__name__,
        cost_estimate=time_cost(6.0),
        compiler_params=params(mib),
    )(run.place, ids[None], part[None], w0, w1, run.tick)
    return out


def capped(k, q):
    t = jnp.tanh(dot_bt(k, q) * (SCALE / CAP))
    return t, jnp.exp(CAP * t)


def levels_kernel(place_ref, own_ref, other_ref, send_ref, near_ref, chip_ref, chip_next_ref):
    core = place_ref[0]
    send_ref[...] = halve(halve(own_ref[...]))
    near_ref[...] = halve(halve(other_ref[...]))
    chip_ref[rows_at(core * 64, 64), :] = halve(send_ref[...])
    chip_ref[rows_at(64 - core * 64, 64), :] = halve(near_ref[...])
    chip_next_ref[...] = halve(chip_ref[...])


def local_forward(place_ref, mine_ref, their_ref, w2_mine_ref, w2_their_ref,
                  q_ref, ga_ref, kl_ref, vl_ref, num_ref, sum_ref):
    for core, (first, second, q_in, ga_in) in (
        (0, (kl_ref, vl_ref, w2_mine_ref, w2_their_ref)),
        (1, (vl_ref, kl_ref, w2_their_ref, w2_mine_ref)),
    ):

        @pl.when(place_ref[0] == core)
        def _(first=first, second=second, q_in=q_in, ga_in=ga_in):
            q_ref[...] = q_in[...]
            ga_ref[...] = ga_in[...]
            for into, rows_in in ((first, mine_ref), (second, their_ref)):
                upper = halve(rows_in[...])
                into[:256, :] = rows_in[:256, :]
                into[256:384, :] = upper[128:, :]
                into[384:640, :] = rows_in[256:, :]
                into[640:, :] = upper[:128, :]

    for h in range(q_ref.shape[1] // DH):
        hs = slice(h * DH, h * DH + DH)
        for pair in range(2):
            rows, keys = slice(pair * 256, pair * 256 + 256), slice(pair * 384, pair * 384 + 384)
            _, e = capped(kl_ref[keys, hs], q_ref[rows, hs])
            w = jnp.concatenate([e[:256], 2.0 * e[256:]], axis=0)
            num_ref[hs, rows] = dot_at(vl_ref[keys, hs], w.astype(BF))
            sum_ref[h : h + 1, rows] = jnp.sum(w, axis=0, keepdims=True)


def far_kernel(place_ref, q_ref, near_mine, near_their, mine_a, mine_b, their_a, their_b, num_ref, sum_ref, ga_ref,
               att_ref, att_keep, att_give, inv_ref, rd_ref, dq_ref, keep_ref, send_ref, kf, vf, dkf, dvf):
    core = place_ref[0]
    for is_core, (mine, their) in ((0, (kf, vf)), (1, (vf, kf))):

        @pl.when(core == is_core)
        def _(mine=mine, their=their):
            for into, near, first, second in ((mine, near_mine, mine_a, mine_b), (their, near_their, their_a, their_b)):
                into[:128, :] = near[...]
                into[128:384, :] = first[...]
                into[384:, :] = second[...]

    for h in range(q_ref.shape[1] // DH):
        hs = slice(h * DH, h * DH + DH)
        q, k, v, ga = q_ref[:, hs], kf[:, hs], vf[:, hs], ga_ref[:, hs]
        t, e = capped(k, q)
        w = jnp.concatenate([e[n * 128 : n * 128 + 128] * float(4 << n) for n in range(5)], axis=0)
        inv = 1.0 / (sum_ref[h : h + 1, :] + jnp.sum(w, axis=0, keepdims=True))
        att = ((num_ref[hs, :] + dot_at(v, w.astype(BF))) * inv).T.astype(BF)
        att_ref[:, hs] = att
        rd = jnp.sum((ga.astype(F32) * att.astype(F32)).T, axis=0, keepdims=True)
        inv_ref[h : h + 1, :] = inv
        rd_ref[h : h + 1, :] = rd
        p = w * inv
        dvf[:, hs] = dot(p.astype(BF), ga)
        g = (p * (dot_bt(v, ga) - rd) * (1.0 - t * t)).astype(BF)
        dq_ref[hs, :] = dot_at(k, g)
        dkf[:, hs] = dot(g, q) * SCALE

    half = att_keep.shape[1]
    att_keep[...] = att_ref[:, rows_at(core * half, half)]
    att_give[...] = att_ref[:, rows_at(half - core * half, half)]
    send_ref[:128, :] = dkf[:128, :].astype(BF)
    send_ref[128:256, :] = dvf[:128, :].astype(BF)
    for is_core, (keep, give) in ((0, (dkf, dvf)), (1, (dvf, dkf))):

        @pl.when(core == is_core)
        def _(keep=keep, give=give):
            keep_ref[...] = keep[128:, :]
            send_ref[256:, :] = give[128:, :].astype(BF)


def local_backward(place_ref, q_ref, kl_ref, vl_ref, inv_ref, rd_ref, ga_ref, dqf_ref,
                   dq_ref, dq_keep, dq_give, dkv_ref, d1_ref):
    width = q_ref.shape[1]
    for h in range(width // DH):
        hs = slice(h * DH, h * DH + DH)
        hv = slice(width + h * DH, width + h * DH + DH)
        for pair in range(2):
            rows, keys = slice(pair * 256, pair * 256 + 256), slice(pair * 384, pair * 384 + 384)
            other = slice((1 - pair) * 128, (1 - pair) * 128 + 128)
            q, ga, k, v = q_ref[rows, hs], ga_ref[rows, hs], kl_ref[keys, hs], vl_ref[keys, hs]
            t, e = capped(k, q)
            inv = inv_ref[h : h + 1, rows]
            p = jnp.concatenate([e[:256] * inv, e[256:] * (2.0 * inv)], axis=0)
            dv = dot(p.astype(BF), ga)
            g = (p * (dot_bt(v, ga) - rd_ref[h : h + 1, rows]) * (1.0 - t * t)).astype(BF)
            dq_ref[rows, hs] = ((dqf_ref[hs, rows] + dot_at(k, g)) * SCALE).T.astype(BF)
            dk = dot(g, q) * SCALE
            dkv_ref[rows, hs] = dk[:256]
            dkv_ref[rows, hv] = dv[:256]
            d1_ref[other, hs] = dk[256:]
            d1_ref[other, hv] = dv[256:]
    dkv_ref[...] += expand(d1_ref[...])
    core, half = place_ref[0], dq_keep.shape[1]
    dq_keep[...] = dq_ref[:, rows_at(core * half, half)]
    dq_give[...] = dq_ref[:, rows_at(half - core * half, half)]


def out_x(place_ref, own_ref, one_ref, two_ref, three_ref, sets_ref, row_ref, row_next_ref):
    x = place_ref[1]
    odd = x & 1
    sets_ref[:128, :] = one_ref[...]
    sets_ref[rows_at(128 + 64 * odd, 64), :] = two_ref[...]
    sets_ref[rows_at(192 - 64 * odd, 64), :] = three_ref[...]
    for apart, part in ((0, own_ref[...]), (1, halve(one_ref[...])), (2, two_ref[...]), (3, three_ref[...])):
        row_ref[rows_at(32 * (x ^ apart), 32), :] = halve(part)
    row_next_ref[...] = halve(row_ref[...])


def out_z(place_ref, one_ref, two_ref, three_ref, sets_ref):
    odd = place_ref[2] & 1
    sets_ref[:128, :] = one_ref[...]
    sets_ref[rows_at(128 + 64 * odd, 64), :] = two_ref[...]
    sets_ref[rows_at(192 - 64 * odd, 64), :] = three_ref[...]


def back_core(place_ref, keep_ref, got_ref, near_ref, one_ref, two_ref, three_ref):
    odd = place_ref[2] & 1
    near_ref[...] = keep_ref[:256, :] + got_ref[256:512, :].astype(F32)
    one_ref[...] = (keep_ref[256:384, :] + got_ref[512:640, :].astype(F32)).astype(BF)
    for into, first in ((two_ref, odd), (three_ref, 1 - odd)):
        kept = keep_ref[rows_at(384 + 64 * first, 64), :]
        into[...] = (kept + got_ref[rows_at(640 + 64 * first, 64), :].astype(F32)).astype(BF)


def back_z(place_ref, near_ref, one_ref, two_ref, three_ref, own_out, one_out, two_out, three_out, row_ref):
    x = place_ref[1]
    odd = x & 1
    row_ref[...] = one_ref[...].astype(F32) + expand(two_ref[...].astype(F32) + three_ref[...].astype(F32))

    def part(apart):
        return row_ref[rows_at(32 * (x ^ apart), 32), :]

    own_out[...] = part(0)
    one_out[...] = (near_ref[:128, :] + expand(part(1), 2)).astype(BF)
    for into, apart, first in ((two_out, 2, odd), (three_out, 3, 1 - odd)):
        into[...] = (near_ref[rows_at(128 + 64 * first, 64), :] + expand(part(apart))).astype(BF)


def back_x(place_ref, own_ref, one_ref, two_ref, three_ref, keep_ref, send_ref, chip_ref):
    core = place_ref[0]
    pair = two_ref[...].astype(F32) + three_ref[...].astype(F32) + expand(own_ref[...])
    chip_ref[...] = one_ref[...].astype(F32) + expand(pair)
    keep_ref[...] = chip_ref[rows_at(64 * core, 64), :]
    send_ref[...] = chip_ref[rows_at(64 - 64 * core, 64), :].astype(BF)


def back_last(place_ref, keep3_ref, got3_ref, got_ref, dkv_ref, mine_ref, their_ref, keep_ref, give_ref):
    width = keep3_ref.shape[1]
    half = width // 2
    for core in range(2):

        @pl.when(place_ref[0] == core)
        def _(core=core):
            for n in range(2):
                upper = keep3_ref[...] if n == core else got3_ref[...].astype(F32)
                level = got_ref[n * 128 : n * 128 + 128, :].astype(F32) + expand(upper)
                done = (dkv_ref[:, n * width : n * width + width] + expand(level, 2)).astype(BF)
                (mine_ref if n == core else their_ref)[...] = done
                keep_ref[:, n * half : n * half + half] = done[:, core * half : core * half + half]
                give_ref[:, n * half : n * half + half] = done[:, half - core * half : width - core * half]


def write_ring_parts(rank, width, product, two_up, two_down, one_ref, three_ref, own_ref):
    half = two_up.shape[0]
    part = product(rows_at((rank + 2) % 4 * width, width)).astype(BF)
    two_up[...] = part[:half]
    two_down[...] = part[half:]
    one_ref[...] = product(rows_at((rank + 1) % 4 * width, width)).astype(BF)
    three_ref[...] = product(rows_at((rank + 3) % 4 * width, width)).astype(BF)
    own_ref[...] = product(rows_at(rank * width, width))


def attended_parts(place_ref, att_ref, w2_mine, w2_their, *outs):
    for core, w_ref in ((0, w2_their), (1, w2_mine)):

        @pl.when(place_ref[0] == core)
        def _(w_ref=w_ref):
            write_ring_parts(place_ref[3], att_ref.shape[1], lambda rows: dot_bt(att_ref[...], w_ref[rows, :]), *outs)


def input_parts(place_ref, dq_ref, mine_ref, their_ref, w1_mine, w1_their, w2_mine, w2_their, *outs):
    for core, wq_ref in ((0, w2_mine), (1, w2_their)):

        @pl.when(place_ref[0] == core)
        def _(wq_ref=wq_ref):
            def product(rows):
                terms = dot_bt(dq_ref[...], wq_ref[rows, :]) + dot_bt(mine_ref[...], w1_mine[rows, :])
                return terms + dot_bt(their_ref[...], w1_their[rows, :])

            write_ring_parts(place_ref[3], dq_ref.shape[1], product, *outs)


def ring_middle(place_ref, one_ref, three_ref, up_ref, down_ref, up_out, down_out):
    half = up_ref.shape[-2]
    low, high = (..., slice(0, half), slice(None)), (..., slice(half, None), slice(None))
    up_out[low] = (one_ref[low].astype(F32) + up_ref[...].astype(F32)).astype(BF)
    up_out[high] = one_ref[high]
    down_out[low] = three_ref[low]
    down_out[high] = (three_ref[high].astype(F32) + down_ref[...].astype(F32)).astype(BF)


def ring_end(place_ref, own_ref, up_ref, down_ref, out_ref):
    out_ref[...] = (own_ref[...] + up_ref[...].astype(F32) + down_ref[...].astype(F32)).astype(BF)


def ring_shapes(dims):
    rows, cols = dims[-2:]
    half, full = (*dims[:-2], rows // 2, cols), dims
    return [jax.ShapeDtypeStruct(half, BF)] * 2 + [jax.ShapeDtypeStruct(full, BF)] * 2 + [jax.ShapeDtypeStruct(full, F32)]


def ring_start(run, kernel, args, dims, axis, us=1.0):
    two_up, two_down, one, three, own = run(kernel, ring_shapes(dims), args, us=us)
    return shift(two_up, axis, 1), shift(two_down, axis, -1), one, three, own


def ring_go_on(run, ring, axis):
    up, down, one, three, own = ring
    out = jax.ShapeDtypeStruct(one.shape, BF)
    up, down = run(ring_middle, [out] * 2, [one, three, up, down])
    return own, shift(up, axis, 1), shift(down, axis, -1)


def early_terms(place_ref, cot_ref, cot_other, att_keep, att_got, tok_ref, tok_other, dq_keep, dq_got,
                two_up, two_down, one_ref, three_ref, own_ref):
    x = place_ref[1]
    half = att_keep.shape[1]
    for at, lhs, lhs_o, keep, got, two in (
        (0, cot_ref, cot_other, att_keep, att_got, two_up),
        (half, tok_ref, tok_other, dq_keep, dq_got, two_down),
    ):
        grads = jnp.concatenate([keep[...].T, got[...].T], axis=1)
        for by, into, start in ((2, two, 0), (1, one_ref, at), (3, three_ref, at), (0, own_ref, at)):
            column = ((x + by) & 3) * 128
            for pair in range(2):
                blocks = []
                for z in (2 * pair, 2 * pair + 1):
                    cols = rows_at(z * 512 + column, 128)
                    blocks.append(jnp.concatenate([lhs[:, cols], lhs_o[:, cols]], axis=0))
                part = dot(grads, jnp.concatenate(blocks, axis=1)).astype(into.dtype)
                into[2 * pair, start : start + half, :] = part[:, :128]
                into[2 * pair + 1, start : start + half, :] = part[:, 128:]


def late_terms(place_ref, tok_ref, tok_other, keep_ref, got_ref, two_up, two_down, one_ref, three_ref, own_ref):
    z = place_ref[2]
    half = two_up.shape[1]
    grads = jnp.concatenate([keep_ref[...].T, got_ref[...].T], axis=1)
    for by, into in ((2, None), (1, one_ref), (3, three_ref), (0, own_ref)):
        for pair in range(2):
            cols = rows_at(((z + by) & 3) * 512 + pair * 256, 256)
            part = dot(grads, jnp.concatenate([tok_ref[:, cols], tok_other[:, cols]], axis=0))
            for n in range(2):
                block = part[:, n * 128 : n * 128 + 128]
                if into is None:
                    two_up[2 * pair + n] = block[:half].astype(BF)
                    two_down[2 * pair + n] = block[half:].astype(BF)
                else:
                    into[2 * pair + n] = block.astype(into.dtype)


def turn_to_z(place_ref, *refs):
    turn(place_ref[2], *refs)


def turn_to_x(place_ref, *refs):
    turn(place_ref[1], *refs)


def turn(here, own_ref, up_ref, down_ref, two_up, two_down, one_ref, three_ref, own_out):
    half = two_up.shape[0]

    def part(by):
        at = (here + by) & 3
        return own_ref[at] + up_ref[at].astype(F32) + down_ref[at].astype(F32)

    two = part(2).astype(BF)
    two_up[...] = two[:half]
    two_down[...] = two[half:]
    one_ref[...] = part(1).astype(BF)
    three_ref[...] = part(3).astype(BF)
    own_out[...] = part(0)


def by_core(place_ref, total, keep_ref, give_ref, turned):
    core = place_ref[0]
    turned[...] = total.T
    keep_ref[...] = turned[rows_at(core * 64, 64), :]
    give_ref[...] = turned[rows_at(64 - core * 64, 64), :]


def part_sums(place_ref, own_ref, up_ref, down_ref, keep_ref, give_ref, turned):
    by_core(place_ref, own_ref[...] + up_ref[...].astype(F32) + down_ref[...].astype(F32), keep_ref, give_ref, turned)


def last_parts(place_ref, early_keep, early_got, kv_keep, kv_got, out_t, query_out, key_out, value_out):
    half = query_out.shape[1] // 2
    for core in range(2):

        @pl.when(place_ref[0] == core)
        def _(core=core):
            for early, kv, side in ((early_keep, kv_keep, core), (early_got, kv_got, 1 - core)):
                cols = slice(side * half, side * half + half)
                out_t[cols, :] = early[:, :half].T
                query_out[:, cols] = early[:, half:]
                key_out[:, cols] = kv[:, :half]
                value_out[:, cols] = kv[:, half:]


def swap(rows, axis, apart):
    return lax.ppermute(rows, axis, [(i, i ^ apart) for i in range(lax.axis_size(axis))])


def shift(rows, axis, by):
    n = lax.axis_size(axis)
    return lax.ppermute(rows, axis, [(i, (i + by) % n) for i in range(n)])


def body(tokens, cotangent, w_query, w_key, w_value, w_out, seeds):
    core, rank = lax.axis_index("core"), lax.axis_index("head")
    run = Chain(jnp.stack([core, lax.axis_index("x"), lax.axis_index("z"), rank]).astype(jnp.int32))
    rows = tokens.shape[0]
    width = w_query.shape[1]
    square, stats = shape(rows, width, BF), shape(width // DH, rows, F32)
    half_cols, turned = shape(rows, width // 2, BF), shape(width, rows, F32)
    part128, part64 = shape(128, width, BF), shape(64, width, BF)

    tok_other, cot_other = swap(tokens, "core", 1), swap(cotangent, "core", 1)

    w1 = perturb(perturb_same, run, core, rank, w_key, w_value, seeds[1], seeds[2], 10007, 56)
    mine0 = dot(tokens, w1).astype(BF)
    give0 = dot(tok_other, w1).astype(BF)
    their0 = swap(give0, "core", 1)
    w1_other = swap(w1, "core", 1)
    level2, near_mine, chip, chip_next = run(levels_kernel, [part128] * 3 + [part64], [mine0, give0])
    x1, x2, x3 = swap(chip, "x", 1), swap(chip_next, "x", 2), swap(chip_next, "x", 3)
    near_their = swap(level2, "core", 1)

    w2 = perturb(perturb_mixed, run, core, rank, w_query, w_out, seeds[0], seeds[3], 7919, 24)
    mine_a, row, row_next = run(out_x, [shape(256, width, BF), part128, part64], [chip_next, x1, x2, x3])
    z1, z2, z3 = swap(row, "z", 1), swap(row_next, "z", 2), swap(row_next, "z", 3)
    their_a = swap(mine_a, "core", 1)
    mine2 = dot(jnp.where(core == 0, tokens, cotangent), w2).astype(BF)
    give2 = dot(jnp.where(core == 0, tok_other, cot_other), w2).astype(BF)
    their2 = swap(give2, "core", 1)
    w2_other = swap(w2, "core", 1)

    queries, grad_att, kl, vl, num, total = run(
        local_forward, [square] * 2 + [shape(768, width, BF)] * 2 + [turned, stats], [mine0, their0, mine2, their2], us=3.0)
    mine_b = run(out_z, [shape(256, width, BF)], [z1, z2, z3])[0]
    their_b = swap(mine_b, "core", 1)
    att, att_keep, att_give, inv, rd, dq_far, keep, send = run(
        far_kernel,
        [square] + [half_cols] * 2 + [stats] * 2 + [turned, shape(512, width, F32), shape(768, width, BF)],
        [queries, near_mine, near_their, mine_a, mine_b, their_a, their_b, num, total, grad_att],
        [pltpu.VMEM((640, width), BF)] * 2 + [pltpu.VMEM((640, width), F32)] * 2, us=6.0)
    got, att_got = swap(send, "core", 1), swap(att_give, "core", 1)

    near, b1, b2, b3 = run(back_core, [shape(256, width, F32), part128, part64, part64], [keep, got])
    b1, b2, b3 = swap(b1, "z", 1), swap(b2, "z", 2), swap(b3, "z", 3)
    att_ring = ring_start(run, attended_parts, [att, w2, w2_other], (rows, width), "head", us=2.0)
    dq, dq_keep, dq_give, dkv_local = run(
        local_backward, [square, half_cols, half_cols, shape(rows, 2 * width, F32)],
        [queries, kl, vl, inv, rd, grad_att, dq_far], [pltpu.VMEM((256, 2 * width), F32)], us=4.0)
    dq_got = swap(dq_give, "core", 1)
    own, c1, c2, c3 = run(
        back_z, [shape(32, width, F32), part128, part64, part64], [near, b1, b2, b3], [pltpu.VMEM((128, width), F32)])
    c1, c2, c3 = swap(c1, "x", 1), swap(c2, "x", 2), swap(c3, "x", 3)
    early = ring_start(
        run, early_terms, [cotangent, cot_other, att_keep, att_got, tokens, tok_other, dq_keep, dq_got],
        (4, width, 128), "x", us=5.0)
    keep3, send3 = run(back_x, [shape(64, width, F32), part64], [own, c1, c2, c3], [pltpu.VMEM((128, width), F32)])
    got3 = swap(send3, "core", 1)
    att_ring = ring_go_on(run, att_ring, "head")
    dkv_mine, dkv_their, dkv_keep, dkv_give = run(back_last, [square] * 4, [keep3, got3, got, dkv_local])
    dkv_got = swap(dkv_give, "core", 1)
    late = ring_start(run, late_terms, [tokens, tok_other, dkv_keep, dkv_got], (4, width, 128), "z", us=3.0)
    early = ring_go_on(run, early, "x")
    in_ring = ring_start(
        run, input_parts, [dq, dkv_mine, dkv_their, w1, w1_other, w2, w2_other], (rows, width), "head", us=5.0)
    late = ring_go_on(run, late, "z")
    early = ring_start(run, turn_to_z, early, (width, 128), "z")
    in_ring = ring_go_on(run, in_ring, "head")
    attended = run(ring_end, [square], att_ring)[0]
    late = ring_start(run, turn_to_x, late, (width, 128), "x")
    early = ring_go_on(run, early, "z")
    late = ring_go_on(run, late, "x")
    sums = [shape(64, width, F32)] * 2, [pltpu.VMEM((128, width), F32)]
    early_keep, early_give = run(part_sums, sums[0], early, sums[1])
    early_got = swap(early_give, "core", 1)
    grad_tokens = run(ring_end, [square], in_ring)[0]
    late_keep, late_give = run(part_sums, sums[0], late, sums[1])
    late_got = swap(late_give, "core", 1)
    grad_w_out, grad_w_query, grad_w_key, grad_w_value = run(
        last_parts, [shape(width, 64, F32)] + [shape(64, width, F32)] * 3, [early_keep, early_got, late_keep, late_got])
    return (attended, grad_tokens, grad_w_query, grad_w_key, grad_w_value, grad_w_out)


def solution(mesh):
    fine = Mesh(mesh.devices.reshape(4, 4, 2, 4), SEQ + ("head",))
    in_specs = (
        P(SEQ, None),
        P(SEQ, None),
        P(None, "head"),
        P(None, "head"),
        P(None, "head"),
        P("head", None),
        P(),
    )
    out_specs = (P(SEQ, "head"),) * 5 + (P("head", SEQ),)
    return jax.shard_map(body, mesh=fine, in_specs=in_specs, out_specs=out_specs, check_vma=False)
```

```python
import math

import jax
import jax.numpy as jnp
from jax import lax
from jax.experimental import pallas as pl
from jax.experimental.pallas import tpu as pltpu
from jax.sharding import Mesh, PartitionSpec as P

DH = 128
LEAF = 128
PRIME = 32749
CAP = 6.0
HALF_NOISE = 0.5
SCALE = 1.0 / math.sqrt(DH)
BF = jnp.bfloat16
F32 = jnp.float32
SEQ = ("z", "x", "core")
VMEM = pl.BlockSpec(memory_space=pltpu.VMEM)
SMEM = pl.BlockSpec(memory_space=pltpu.SMEM)
HBM = pl.BlockSpec(memory_space=pltpu.HBM)
ANY = pl.BlockSpec(memory_space=pl.ANY)


def params(mib=24):
    return pltpu.CompilerParams(vmem_limit_bytes=mib << 20)


class Chain:
    def __init__(self):
        self.tick = None

    def call(self, kernel, outs, args, specs, scratch, us, mib=24, aliases={}):
        first, used = self.tick is None, len(args)

        def run(*refs):
            ins, tick_in, rest = refs[:used], refs[used : used + 1 - first], refs[used + 1 - first :]
            rest[0][...] = jnp.zeros((1, 128), F32) if first else tick_in[0][...]
            kernel(here(), *ins, *rest[1:])

        ticks = [] if first else [self.tick]
        self.tick, *results = pl.pallas_call(
            run,
            out_shape=[shape(1, 128, F32), *outs],
            in_specs=specs + [VMEM] * len(ticks),
            out_specs=[VMEM] + [ANY if n in aliases else VMEM for n in range(len(outs))],
            scratch_shapes=list(scratch),
            name=kernel.__name__,
            input_output_aliases={n: 1 + n for n in aliases},
            cost_estimate=pl.CostEstimate(flops=int(us * 1e9), bytes_accessed=1, transcendentals=0),
            compiler_params=params(mib),
        )(*args, *ticks)
        return results

    def __call__(self, kernel, outs, args, scratch=(), us=1.0):
        return self.call(kernel, outs, args, [VMEM] * len(args), scratch, us)

    def hold(self, *arrays):
        return self.call(
            wait_here, [jax.ShapeDtypeStruct(a.shape, a.dtype) for a in arrays], arrays, [ANY] * len(arrays), (), 0.1,
            aliases=range(len(arrays)))


def wait_here(place, *refs):
    pass


def here():
    return [lax.axis_index(name) for name in ("core", "x", "z", "head")]


def shape(rows, cols, dtype):
    return jax.ShapeDtypeStruct((rows, cols), dtype)


def dot(a, b):
    return jnp.dot(a, b, preferred_element_type=F32)


def dot_bt(a, b):
    return lax.dot_general(a, b, (((1,), (1,)), ((), ())), preferred_element_type=F32)


def dot_at(a, b):
    return lax.dot_general(a, b, (((0,), (0,)), ((), ())), preferred_element_type=F32)


def rows_at(start, count):
    return pl.ds(pl.multiple_of(start, count), count)


def halve(rows_in):
    rows = rows_in.shape[0]
    out_row = lax.broadcasted_iota(jnp.int32, (rows // 2, rows), 0)
    in_row = lax.broadcasted_iota(jnp.int32, (rows // 2, rows), 1)
    average = jnp.where(lax.shift_right_logical(in_row, 1) == out_row, 0.5, 0.0).astype(BF)
    return dot(average, rows_in).astype(BF)


def expand(rows_in, shift=1):
    rows, times = rows_in.shape[0], 1 << shift
    out_row = lax.broadcasted_iota(jnp.int32, (rows * times, rows), 0)
    in_row = lax.broadcasted_iota(jnp.int32, (rows * times, rows), 1)
    spread = jnp.where(lax.shift_right_logical(out_row, shift) == in_row, 1.0 / times, 0.0).astype(BF)
    high = rows_in.astype(BF)
    low = (rows_in - high.astype(F32)).astype(BF)
    return dot(spread, high) + dot(spread, low)


def fold(value):
    for _ in range(2):
        value = lax.shift_right_logical(value, 15) * 19 + (value & 32767)
    return value


def below_prime(value):
    return jnp.where(value >= PRIME, value - PRIME, value)


def hash_of(row_part, col_part, row_ids, col_ids):
    h = row_part + col_part
    f = h.astype(F32)
    quotient = (f * (f * (1.0 / PRIME))).astype(jnp.int32)
    h = h * h - quotient * PRIME + col_ids
    return below_prime(fold(h * h + row_ids)).astype(F32)


def noise_all(w_ref, out_ref, rank, seed, lanes_are_rows):
    rows, cols = w_ref.shape
    chunk = 64
    mult, lane_mult = (10007, 7919) if lanes_are_rows else (7919, 10007)
    own_ids = lax.broadcasted_iota(jnp.int32, (1, cols), 1) + rank * cols
    own_part = below_prime(below_prime(fold(own_ids * lane_mult)) + below_prime(fold(seed * 31337)))

    def add_squares(i, acc):
        w = w_ref[rows_at(i * 64, 64), :].astype(F32)
        return acc + jnp.sum((w * w).reshape(8, 8, cols), axis=0)

    acc = lax.fori_loop(0, rows // 64, add_squares, jnp.zeros((8, cols), F32))
    mean = jnp.sum(acc, axis=0, keepdims=True) * (1.0 / rows)
    amp = HALF_NOISE * jnp.sqrt(mean + 1e-06)
    slope = amp * (2.0 / (PRIME - 1))

    def step(i, carry):
        ids, part = carry
        for lane in range(cols // 128):
            here = slice(lane * 128, lane * 128 + 128)
            lane_ids, lane_part = own_ids[:, here], own_part[:, here]
            if lanes_are_rows:
                hashed = hash_of(lane_part, part, lane_ids, ids)
            else:
                hashed = hash_of(part, lane_part, ids, lane_ids)
            w = w_ref[rows_at(i * chunk, chunk), here].astype(F32)
            out_ref[rows_at(i * chunk, chunk), here] = ((w - amp[:, here]) + slope[:, here] * hashed).astype(BF)
        return ids + chunk, below_prime(part + chunk * mult % PRIME)

    ids = lax.broadcasted_iota(jnp.int32, (chunk, 128), 0)
    lax.fori_loop(0, rows // chunk, step, (ids, ids * mult % PRIME))


def perturb_one(w_from, x_from, seed, rank, out_ref, own_ref, w_ref, x_ref, sems, by_rows):
    rows = x_from.shape[0]
    x_copy = pltpu.make_async_copy(x_from, x_ref, sems.at[4])
    pieces = w_ref.shape[0] // 4
    copies = [
        pltpu.make_async_copy(w_from.at[n * pieces : n * pieces + pieces, :], w_ref.at[n * pieces : n * pieces + pieces, :], sems.at[n])
        for n in range(4)
    ]
    for copy in copies:
        copy.start()
    x_copy.start()
    for copy in copies:
        copy.wait()
    if by_rows is not None:
        for n in range(by_rows.shape[0] // 128):
            by_rows[n * 128 : n * 128 + 128, :] = w_ref[:, n * 128 : n * 128 + 128].T
        w_ref = by_rows
    noise_all(w_ref, out_ref, rank, seed, by_rows is not None)
    x_copy.wait()
    for n in range(2):
        part = slice(n * rows // 2, n * rows // 2 + rows // 2)
        own_ref[part, :] = dot(x_ref[part, :], out_ref[...]).astype(BF)


def perturb_same(place, seeds_ref, w0_ref, w1_ref, x_from, out_ref, own_ref, w_ref, x_ref, sems):
    for core, w_from in ((0, w0_ref), (1, w1_ref)):

        @pl.when(place[0] == core)
        def _(core=core, w_from=w_from):
            perturb_one(w_from, x_from, seeds_ref[1 + core], place[3], out_ref, own_ref, w_ref, x_ref, sems, None)


def perturb_mixed(place, seeds_ref, w0_ref, w1_ref, x0_from, x1_from, out_ref, own_ref, w_ref, x_ref, sems, wide_ref):
    @pl.when(place[0] == 0)
    def _():
        perturb_one(w0_ref, x0_from, seeds_ref[0], place[3], out_ref, own_ref, w_ref, x_ref, sems, None)

    @pl.when(place[0] == 1)
    def _():
        perturb_one(w1_ref, x1_from, seeds_ref[3], place[3], out_ref, own_ref, wide_ref, x_ref, sems, w_ref)


def perturb(run, kernel, seeds, w0, w1, activations, mib):
    rows, cols = w0.shape
    tokens = activations[0].shape
    wide = [pltpu.VMEM(w1.shape, BF)] if w1.shape != w0.shape else []
    return run.call(
        kernel, [shape(rows, cols, BF), shape(tokens[0], cols, BF)], [seeds, w0, w1, *activations],
        [SMEM] + [HBM] * (2 + len(activations)),
        [pltpu.VMEM((rows, cols), BF), pltpu.VMEM(tokens, BF), pltpu.SemaphoreType.DMA((5,))] + wide, 7.0, mib)


def capped(k, q):
    t = jnp.tanh(dot_bt(k, q) * (SCALE / CAP))
    return t, jnp.exp(CAP * t)


def levels_kernel(place, own_ref, other_ref, send_ref, near_ref, chip_ref, chip_next_ref):
    core = place[0]
    send_ref[...] = halve(halve(own_ref[...]))
    near_ref[...] = halve(halve(other_ref[...]))
    chip_ref[rows_at(core * 64, 64), :] = halve(send_ref[...])
    chip_ref[rows_at(64 - core * 64, 64), :] = halve(near_ref[...])
    chip_next_ref[...] = halve(chip_ref[...])


def local_forward(place, mine_ref, their_ref, w2_mine_ref, w2_their_ref,
                  q_ref, ga_ref, kl_ref, vl_ref, num_ref, sum_ref):
    for core, (first, second, q_in, ga_in) in (
        (0, (kl_ref, vl_ref, w2_mine_ref, w2_their_ref)),
        (1, (vl_ref, kl_ref, w2_their_ref, w2_mine_ref)),
    ):

        @pl.when(place[0] == core)
        def _(first=first, second=second, q_in=q_in, ga_in=ga_in):
            q_ref[...] = q_in[...]
            ga_ref[...] = ga_in[...]
            for into, rows_in in ((first, mine_ref), (second, their_ref)):
                upper = halve(rows_in[...])
                into[:256, :] = rows_in[:256, :]
                into[256:384, :] = upper[128:, :]
                into[384:640, :] = rows_in[256:, :]
                into[640:, :] = upper[:128, :]

    for h in range(q_ref.shape[1] // DH):
        hs = slice(h * DH, h * DH + DH)
        for pair in range(2):
            rows, keys = slice(pair * 256, pair * 256 + 256), slice(pair * 384, pair * 384 + 384)
            _, e = capped(kl_ref[keys, hs], q_ref[rows, hs])
            w = jnp.concatenate([e[:256], 2.0 * e[256:]], axis=0)
            num_ref[hs, rows] = dot_at(vl_ref[keys, hs], w.astype(BF))
            sum_ref[h : h + 1, rows] = jnp.sum(w, axis=0, keepdims=True)


def far_kernel(place, q_ref, near_mine, near_their, mine_a, mine_b, their_a, their_b, num_ref, sum_ref, ga_ref,
               att_ref, att_keep, att_give, inv_ref, rd_ref, dq_ref, keep_ref, send_ref, kf, vf, dkf, dvf):
    core = place[0]
    for is_core, (mine, their) in ((0, (kf, vf)), (1, (vf, kf))):

        @pl.when(core == is_core)
        def _(mine=mine, their=their):
            for into, near, first, second in ((mine, near_mine, mine_a, mine_b), (their, near_their, their_a, their_b)):
                into[:128, :] = near[...]
                into[128:384, :] = first[...]
                into[384:, :] = second[...]

    for h in range(q_ref.shape[1] // DH):
        hs = slice(h * DH, h * DH + DH)
        q, k, v, ga = q_ref[:, hs], kf[:, hs], vf[:, hs], ga_ref[:, hs]
        t, e = capped(k, q)
        w = jnp.concatenate([e[n * 128 : n * 128 + 128] * float(4 << n) for n in range(5)], axis=0)
        inv = 1.0 / (sum_ref[h : h + 1, :] + jnp.sum(w, axis=0, keepdims=True))
        att = ((num_ref[hs, :] + dot_at(v, w.astype(BF))) * inv).T.astype(BF)
        att_ref[:, hs] = att
        rd = jnp.sum((ga.astype(F32) * att.astype(F32)).T, axis=0, keepdims=True)
        inv_ref[h : h + 1, :] = inv
        rd_ref[h : h + 1, :] = rd
        p = w * inv
        dvf[:, hs] = dot(p.astype(BF), ga)
        g = (p * (dot_bt(v, ga) - rd) * (1.0 - t * t)).astype(BF)
        dq_ref[hs, :] = dot_at(k, g)
        dkf[:, hs] = dot(g, q) * SCALE

    half = att_keep.shape[1]
    att_keep[...] = att_ref[:, rows_at(core * half, half)]
    att_give[...] = att_ref[:, rows_at(half - core * half, half)]
    send_ref[:128, :] = dkf[:128, :].astype(BF)
    send_ref[128:256, :] = dvf[:128, :].astype(BF)
    for is_core, (keep, give) in ((0, (dkf, dvf)), (1, (dvf, dkf))):

        @pl.when(core == is_core)
        def _(keep=keep, give=give):
            keep_ref[...] = keep[128:, :]
            send_ref[256:, :] = give[128:, :].astype(BF)


def local_backward(place, q_ref, kl_ref, vl_ref, inv_ref, rd_ref, ga_ref, dqf_ref,
                   dq_ref, dq_keep, dq_give, dkv_ref, d1_ref):
    width = q_ref.shape[1]
    for h in range(width // DH):
        hs = slice(h * DH, h * DH + DH)
        hv = slice(width + h * DH, width + h * DH + DH)
        for pair in range(2):
            rows, keys = slice(pair * 256, pair * 256 + 256), slice(pair * 384, pair * 384 + 384)
            other = slice((1 - pair) * 128, (1 - pair) * 128 + 128)
            q, ga, k, v = q_ref[rows, hs], ga_ref[rows, hs], kl_ref[keys, hs], vl_ref[keys, hs]
            t, e = capped(k, q)
            inv = inv_ref[h : h + 1, rows]
            p = jnp.concatenate([e[:256] * inv, e[256:] * (2.0 * inv)], axis=0)
            dv = dot(p.astype(BF), ga)
            g = (p * (dot_bt(v, ga) - rd_ref[h : h + 1, rows]) * (1.0 - t * t)).astype(BF)
            dq_ref[rows, hs] = ((dqf_ref[hs, rows] + dot_at(k, g)) * SCALE).T.astype(BF)
            dk = dot(g, q) * SCALE
            dkv_ref[rows, hs] = dk[:256]
            dkv_ref[rows, hv] = dv[:256]
            d1_ref[other, hs] = dk[256:]
            d1_ref[other, hv] = dv[256:]
    dkv_ref[...] += expand(d1_ref[...])
    core, half = place[0], dq_keep.shape[1]
    dq_keep[...] = dq_ref[:, rows_at(core * half, half)]
    dq_give[...] = dq_ref[:, rows_at(half - core * half, half)]


def out_x(place, own_ref, one_ref, two_ref, three_ref, sets_ref, row_ref, row_next_ref):
    x = place[1]
    odd = x & 1
    sets_ref[:128, :] = one_ref[...]
    sets_ref[rows_at(128 + 64 * odd, 64), :] = two_ref[...]
    sets_ref[rows_at(192 - 64 * odd, 64), :] = three_ref[...]
    for apart, part in ((0, own_ref[...]), (1, halve(one_ref[...])), (2, two_ref[...]), (3, three_ref[...])):
        row_ref[rows_at(32 * (x ^ apart), 32), :] = halve(part)
    row_next_ref[...] = halve(row_ref[...])


def out_z(place, one_ref, two_ref, three_ref, sets_ref):
    odd = place[2] & 1
    sets_ref[:128, :] = one_ref[...]
    sets_ref[rows_at(128 + 64 * odd, 64), :] = two_ref[...]
    sets_ref[rows_at(192 - 64 * odd, 64), :] = three_ref[...]


def back_core(place, keep_ref, got_ref, near_ref, one_ref, two_ref, three_ref):
    odd = place[2] & 1
    near_ref[...] = keep_ref[:256, :] + got_ref[256:512, :].astype(F32)
    one_ref[...] = (keep_ref[256:384, :] + got_ref[512:640, :].astype(F32)).astype(BF)
    for into, first in ((two_ref, odd), (three_ref, 1 - odd)):
        kept = keep_ref[rows_at(384 + 64 * first, 64), :]
        into[...] = (kept + got_ref[rows_at(640 + 64 * first, 64), :].astype(F32)).astype(BF)


def back_z(place, near_ref, one_ref, two_ref, three_ref, own_out, one_out, two_out, three_out, row_ref):
    x = place[1]
    odd = x & 1
    row_ref[...] = one_ref[...].astype(F32) + expand(two_ref[...].astype(F32) + three_ref[...].astype(F32))

    def part(apart):
        return row_ref[rows_at(32 * (x ^ apart), 32), :]

    own_out[...] = part(0)
    one_out[...] = (near_ref[:128, :] + expand(part(1), 2)).astype(BF)
    for into, apart, first in ((two_out, 2, odd), (three_out, 3, 1 - odd)):
        into[...] = (near_ref[rows_at(128 + 64 * first, 64), :] + expand(part(apart))).astype(BF)


def back_x(place, own_ref, one_ref, two_ref, three_ref, keep_ref, send_ref, chip_ref):
    core = place[0]
    pair = two_ref[...].astype(F32) + three_ref[...].astype(F32) + expand(own_ref[...])
    chip_ref[...] = one_ref[...].astype(F32) + expand(pair)
    keep_ref[...] = chip_ref[rows_at(64 * core, 64), :]
    send_ref[...] = chip_ref[rows_at(64 - 64 * core, 64), :].astype(BF)


def back_last(place, keep3_ref, got3_ref, got_ref, dkv_ref, mine_ref, their_ref, keep_ref, give_ref):
    width = keep3_ref.shape[1]
    half = width // 2
    for core in range(2):

        @pl.when(place[0] == core)
        def _(core=core):
            for n in range(2):
                upper = keep3_ref[...] if n == core else got3_ref[...].astype(F32)
                level = got_ref[n * 128 : n * 128 + 128, :].astype(F32) + expand(upper)
                done = (dkv_ref[:, n * width : n * width + width] + expand(level, 2)).astype(BF)
                (mine_ref if n == core else their_ref)[...] = done
                keep_ref[:, n * half : n * half + half] = done[:, core * half : core * half + half]
                give_ref[:, n * half : n * half + half] = done[:, half - core * half : width - core * half]


def part_shapes(*dims):
    return [jax.ShapeDtypeStruct(dims, F32)] + [jax.ShapeDtypeStruct(dims, BF)] * 3


def send_parts(parts, axis):
    own, one, two, three = parts
    return own, shift(one, axis, 1), shift(two, axis, 2), shift(three, axis, -1)


def total(own, one, two, three):
    return own + one.astype(F32) + two.astype(F32) + three.astype(F32)


def write_parts(rank, width, product, outs):
    for by, into in enumerate(outs):
        into[...] = product(rows_at(((rank + by) & 3) * width, width)).astype(into.dtype)


def attended_parts(place, att_ref, w2_mine, w2_their, *outs):
    for core, w_ref in ((0, w2_their), (1, w2_mine)):

        @pl.when(place[0] == core)
        def _(w_ref=w_ref):
            write_parts(place[3], att_ref.shape[1], lambda rows: dot_bt(att_ref[...], w_ref[rows, :]), outs)


def input_parts(place, dq_ref, mine_ref, their_ref, w1_mine, w1_their, w2_mine, w2_their, *outs):
    for core, wq_ref in ((0, w2_mine), (1, w2_their)):

        @pl.when(place[0] == core)
        def _(wq_ref=wq_ref):
            def product(rows):
                terms = dot_bt(dq_ref[...], wq_ref[rows, :]) + dot_bt(mine_ref[...], w1_mine[rows, :])
                return terms + dot_bt(their_ref[...], w1_their[rows, :])

            write_parts(place[3], dq_ref.shape[1], product, outs)


def parts_end(place, own_ref, one_ref, two_ref, three_ref, out_ref):
    out_ref[...] = total(own_ref[...], one_ref[...], two_ref[...], three_ref[...]).astype(BF)


def gradient_blocks(lhs, lhs_other, keep, got, cols):
    grads = jnp.concatenate([keep[...].T, got[...].T], axis=1)
    rows = [jnp.concatenate([lhs[:, c], lhs_other[:, c]], axis=0) for c in cols]
    return dot(grads, jnp.concatenate(rows, axis=1))


def early_terms(place, cot, cot_other, att_keep, att_got, tok, tok_other, dq_keep, dq_got, *outs):
    half = att_keep.shape[1]
    for at, sources in ((0, (cot, cot_other, att_keep, att_got)), (half, (tok, tok_other, dq_keep, dq_got))):
        for by, into in enumerate(outs):
            for pair in range(2):
                cols = [rows_at((2 * pair + n) * 512 + ((place[1] + by) & 3) * 128, 128) for n in range(2)]
                part = gradient_blocks(*sources, cols).astype(into.dtype)
                for n in range(2):
                    into[2 * pair + n, at : at + half, :] = part[:, n * 128 : n * 128 + 128]


def late_terms(place, tok, tok_other, keep, got, *outs):
    for by, into in enumerate(outs):
        for pair in range(2):
            cols = [rows_at(((place[2] + by) & 3) * 512 + pair * 256, 256)]
            part = gradient_blocks(tok, tok_other, keep, got, cols).astype(into.dtype)
            for n in range(2):
                into[2 * pair + n] = part[:, n * 128 : n * 128 + 128]


def turn_to_z(place, *refs):
    turn(place[2], *refs)


def turn_to_x(place, *refs):
    turn(place[1], *refs)


def turn(at, own_ref, one_ref, two_ref, three_ref, *outs):
    for by, into in enumerate(outs):
        n = (at + by) & 3
        into[...] = total(own_ref[n], one_ref[n], two_ref[n], three_ref[n]).astype(into.dtype)


def chip_sums(place, *refs):
    early, late, (keep_ref, give_ref, turned) = refs[:4], refs[4:8], refs[8:]
    width = early[0].shape[0]
    for n, parts in enumerate((early, late)):
        turned[:, n * width : n * width + width] = total(*(r[...] for r in parts)).T
    keep_ref[...] = turned[rows_at(place[0] * 64, 64), :]
    give_ref[...] = turned[rows_at(64 - place[0] * 64, 64), :]


def last_parts(place, keep_ref, got_ref, *outs):
    half = outs[0].shape[1] // 2
    for core in range(2):

        @pl.when(place[0] == core)
        def _(core=core):
            for from_ref, side in ((keep_ref, core), (got_ref, 1 - core)):
                for n, into in enumerate(outs):
                    into[:, side * half : side * half + half] = from_ref[:, n * half : n * half + half]


def swap(rows, axis, apart):
    return lax.ppermute(rows, axis, [(i, i ^ apart) for i in range(lax.axis_size(axis))])


def shift(rows, axis, by):
    n = lax.axis_size(axis)
    return lax.ppermute(rows, axis, [(i, (i + by) % n) for i in range(n)])


def body(tokens, cotangent, w_query, w_key, w_value, w_out, seeds):
    run = Chain()
    core = lax.axis_index("core")
    rows = tokens.shape[0]
    width = w_query.shape[1]
    square, stats = shape(rows, width, BF), shape(width // DH, rows, F32)
    half_cols, turned = shape(rows, width // 2, BF), shape(width, rows, F32)
    part128, part64 = shape(128, width, BF), shape(64, width, BF)

    tok_other, cot_other = swap(tokens, "core", 1), swap(cotangent, "core", 1)

    w1, mine0 = perturb(run, perturb_same, seeds, w_key, w_value, [tokens], 56)
    give0 = dot(tok_other, w1).astype(BF)
    their0 = swap(give0, "core", 1)
    cot_other = run.hold(cot_other)[0]
    level2, near_mine, chip, chip_next = run(levels_kernel, [part128] * 3 + [part64], [mine0, give0])
    x1, x2, x3 = swap(chip, "x", 1), swap(chip_next, "x", 2), swap(chip_next, "x", 3)
    near_their = swap(level2, "core", 1)
    their0, near_their = run.hold(their0, near_their)

    w2, mine2 = perturb(run, perturb_mixed, seeds, w_query, w_out, [tokens, cotangent], 56)
    mine_a, row, row_next = run(out_x, [shape(256, width, BF), part128, part64], [chip_next, x1, x2, x3])
    z1, z2, z3 = swap(row, "z", 1), swap(row_next, "z", 2), swap(row_next, "z", 3)
    their_a = swap(mine_a, "core", 1)
    w2 = run.hold(w2)[0]
    give2 = dot(jnp.where(core == 0, tok_other, cot_other), w2).astype(BF)
    their2 = swap(give2, "core", 1)
    their_a = run.hold(their_a)[0]

    queries, grad_att, kl, vl, num, total = run(
        local_forward, [square] * 2 + [shape(768, width, BF)] * 2 + [turned, stats], [mine0, their0, mine2, their2], us=3.0)
    mine_b = run(out_z, [shape(256, width, BF)], [z1, z2, z3])[0]
    their_b = swap(mine_b, "core", 1)
    att, att_keep, att_give, inv, rd, dq_far, keep, send = run(
        far_kernel,
        [square] + [half_cols] * 2 + [stats] * 2 + [turned, shape(512, width, F32), shape(768, width, BF)],
        [queries, near_mine, near_their, mine_a, mine_b, their_a, their_b, num, total, grad_att],
        [pltpu.VMEM((640, width), BF)] * 2 + [pltpu.VMEM((640, width), F32)] * 2, us=6.0)
    got, att_got = swap(send, "core", 1), swap(att_give, "core", 1)

    near, b1, b2, b3 = run(back_core, [shape(256, width, F32), part128, part64, part64], [keep, got])
    w2, att_got = run.hold(w2, att_got)
    w2_other = swap(w2, "core", 1)
    b1, b2, b3 = swap(b1, "z", 1), swap(b2, "z", 2), swap(b3, "z", 3)
    dq, dq_keep, dq_give, dkv_local = run(
        local_backward, [square, half_cols, half_cols, shape(rows, 2 * width, F32)],
        [queries, kl, vl, inv, rd, grad_att, dq_far], [pltpu.VMEM((256, 2 * width), F32)], us=4.0)
    own, c1, c2, c3 = run(
        back_z, [shape(32, width, F32), part128, part64, part64], [near, b1, b2, b3], [pltpu.VMEM((128, width), F32)])
    c1, c2, c3 = swap(c1, "x", 1), swap(c2, "x", 2), swap(c3, "x", 3)
    dq_give, w2_other, w1 = run.hold(dq_give, w2_other, w1)
    dq_got, w1_other = swap(dq_give, "core", 1), swap(w1, "core", 1)
    att_parts = run(attended_parts, part_shapes(rows, width), [att, w2, w2_other], us=2.0)
    early = run(
        early_terms, part_shapes(4, width, 128),
        [cotangent, cot_other, att_keep, att_got, tokens, tok_other, dq_keep, dq_got], us=5.0)
    keep3, send3 = run(back_x, [shape(64, width, F32), part64], [own, c1, c2, c3], [pltpu.VMEM((128, width), F32)])
    got3 = swap(send3, "core", 1)
    att_parts = send_parts(run.hold(*att_parts), "head")
    dkv_mine, dkv_their, dkv_keep, dkv_give = run(back_last, [square] * 4, [keep3, got3, got, dkv_local])
    dkv_got = swap(dkv_give, "core", 1)
    early = send_parts(run.hold(*early), "x")
    late = run(late_terms, part_shapes(4, width, 128), [tokens, tok_other, dkv_keep, dkv_got], us=3.0)
    late = send_parts(late, "z")
    in_parts = run(input_parts, part_shapes(rows, width),
                   [dq, dkv_mine, dkv_their, w1, w1_other, w2, w2_other], us=5.0)
    attended = run(parts_end, [square], att_parts)[0]
    in_parts = send_parts(in_parts, "head")
    early = send_parts(run(turn_to_z, part_shapes(width, 128), early), "z")
    late = send_parts(run(turn_to_x, part_shapes(width, 128), late), "x")
    grad_tokens = run(parts_end, [square], in_parts)[0]
    keep, give = run(chip_sums, [shape(64, 2 * width, F32)] * 2, [*early, *late], [pltpu.VMEM((128, 2 * width), F32)])
    grad_w_out, grad_w_query, grad_w_key, grad_w_value = run(
        last_parts, [shape(64, width, F32)] * 4, [keep, swap(give, "core", 1)])
    return (attended, grad_tokens, grad_w_query, grad_w_key, grad_w_value, grad_w_out.T)


def solution(mesh):
    fine = Mesh(mesh.devices.reshape(4, 4, 2, 4), SEQ + ("head",))
    in_specs = (
        P(SEQ, None),
        P(SEQ, None),
        P(None, "head"),
        P(None, "head"),
        P(None, "head"),
        P("head", None),
        P(),
    )
    out_specs = (P(SEQ, "head"),) * 5 + (P("head", SEQ),)
    return jax.shard_map(body, mesh=fine, in_specs=in_specs, out_specs=out_specs, check_vma=False)
```

```python
import math

import jax
import jax.numpy as jnp
from jax import lax
from jax.experimental import pallas as pl
from jax.experimental.pallas import tpu as pltpu
from jax.sharding import Mesh, PartitionSpec as P

DH = 128
LEAF = 128
PRIME = 32749
CAP = 6.0
HALF_NOISE = 0.5
SCALE = 1.0 / math.sqrt(DH)
BF = jnp.bfloat16
F32 = jnp.float32
SEQ = ("z", "x", "core")
VMEM = pl.BlockSpec(memory_space=pltpu.VMEM)
SMEM = pl.BlockSpec(memory_space=pltpu.SMEM)
HBM = pl.BlockSpec(memory_space=pltpu.HBM)
ANY = pl.BlockSpec(memory_space=pl.ANY)


def params(mib=24):
    return pltpu.CompilerParams(vmem_limit_bytes=mib << 20)


class Chain:
    def __init__(self):
        self.tick = None

    def call(self, kernel, outs, args, specs, scratch, us, mib=24, aliases={}):
        first, used = self.tick is None, len(args)

        def run(*refs):
            ins, tick_in, rest = refs[:used], refs[used : used + 1 - first], refs[used + 1 - first :]
            rest[0][...] = jnp.zeros((1, 128), F32) if first else tick_in[0][...]
            kernel(here(), *ins, *rest[1:])

        ticks = [] if first else [self.tick]
        self.tick, *results = pl.pallas_call(
            run,
            out_shape=[shape(1, 128, F32), *outs],
            in_specs=specs + [VMEM] * len(ticks),
            out_specs=[VMEM] + [ANY if n in aliases else VMEM for n in range(len(outs))],
            scratch_shapes=list(scratch),
            name=kernel.__name__,
            input_output_aliases={n: 1 + n for n in aliases},
            cost_estimate=pl.CostEstimate(flops=int(us * 1e9), bytes_accessed=1, transcendentals=0),
            compiler_params=params(mib),
        )(*args, *ticks)
        return results

    def __call__(self, kernel, outs, args, scratch=(), us=1.0):
        return self.call(kernel, outs, args, [VMEM] * len(args), scratch, us)

    def hold(self, *arrays):
        return self.call(
            wait_here, [jax.ShapeDtypeStruct(a.shape, a.dtype) for a in arrays], arrays, [ANY] * len(arrays), (), 0.1,
            aliases=range(len(arrays)))


def wait_here(place, *refs):
    pass


def here():
    return [lax.axis_index(name) for name in ("core", "x", "z", "head")]


def shape(rows, cols, dtype):
    return jax.ShapeDtypeStruct((rows, cols), dtype)


def dot(a, b):
    return jnp.dot(a, b, preferred_element_type=F32)


def dot_bt(a, b):
    return lax.dot_general(a, b, (((1,), (1,)), ((), ())), preferred_element_type=F32)


def dot_at(a, b):
    return lax.dot_general(a, b, (((0,), (0,)), ((), ())), preferred_element_type=F32)


def rows_at(start, count):
    return pl.ds(pl.multiple_of(start, count), count)


def halve(rows_in):
    rows = rows_in.shape[0]
    out_row = lax.broadcasted_iota(jnp.int32, (rows // 2, rows), 0)
    in_row = lax.broadcasted_iota(jnp.int32, (rows // 2, rows), 1)
    average = jnp.where(lax.shift_right_logical(in_row, 1) == out_row, 0.5, 0.0).astype(BF)
    return dot(average, rows_in).astype(BF)


def expand(rows_in, shift=1):
    rows, times = rows_in.shape[0], 1 << shift
    out_row = lax.broadcasted_iota(jnp.int32, (rows * times, rows), 0)
    in_row = lax.broadcasted_iota(jnp.int32, (rows * times, rows), 1)
    spread = jnp.where(lax.shift_right_logical(out_row, shift) == in_row, 1.0 / times, 0.0).astype(BF)
    high = rows_in.astype(BF)
    low = (rows_in - high.astype(F32)).astype(BF)
    return dot(spread, high) + dot(spread, low)


def fold(value):
    for _ in range(2):
        value = lax.shift_right_logical(value, 15) * 19 + (value & 32767)
    return value


def below_prime(value):
    return jnp.where(value >= PRIME, value - PRIME, value)


def hash_of(row_part, col_part, row_ids, col_ids):
    h = row_part + col_part
    f = h.astype(F32)
    quotient = (f * (f * (1.0 / PRIME))).astype(jnp.int32)
    h = h * h - quotient * PRIME + col_ids
    return below_prime(fold(h * h + row_ids)).astype(F32)


def noise_all(w_ref, out_ref, rank, seed, lanes_are_rows):
    rows, cols = w_ref.shape
    chunk = 64
    mult, lane_mult = (10007, 7919) if lanes_are_rows else (7919, 10007)
    own_ids = lax.broadcasted_iota(jnp.int32, (1, cols), 1) + rank * cols
    own_part = below_prime(below_prime(fold(own_ids * lane_mult)) + below_prime(fold(seed * 31337)))

    def add_squares(i, acc):
        w = w_ref[rows_at(i * 64, 64), :].astype(F32)
        return acc + jnp.sum((w * w).reshape(8, 8, cols), axis=0)

    acc = lax.fori_loop(0, rows // 64, add_squares, jnp.zeros((8, cols), F32))
    mean = jnp.sum(acc, axis=0, keepdims=True) * (1.0 / rows)
    amp = HALF_NOISE * jnp.sqrt(mean + 1e-06)
    slope = amp * (2.0 / (PRIME - 1))

    def step(i, carry):
        ids, part = carry
        for lane in range(cols // 128):
            here = slice(lane * 128, lane * 128 + 128)
            lane_ids, lane_part = own_ids[:, here], own_part[:, here]
            if lanes_are_rows:
                hashed = hash_of(lane_part, part, lane_ids, ids)
            else:
                hashed = hash_of(part, lane_part, ids, lane_ids)
            w = w_ref[rows_at(i * chunk, chunk), here].astype(F32)
            out_ref[rows_at(i * chunk, chunk), here] = ((w - amp[:, here]) + slope[:, here] * hashed).astype(BF)
        return ids + chunk, below_prime(part + chunk * mult % PRIME)

    ids = lax.broadcasted_iota(jnp.int32, (chunk, 128), 0)
    lax.fori_loop(0, rows // chunk, step, (ids, ids * mult % PRIME))


def perturb_one(w_from, x_from, seed, rank, out_ref, own_ref, w_ref, x_ref, sems, by_rows):
    rows = x_from.shape[0]
    x_copy = pltpu.make_async_copy(x_from, x_ref, sems.at[8])
    pieces = w_ref.shape[0] // 8
    copies = [
        pltpu.make_async_copy(w_from.at[n * pieces : n * pieces + pieces, :], w_ref.at[n * pieces : n * pieces + pieces, :], sems.at[n])
        for n in range(8)
    ]
    for copy in copies:
        copy.start()
    for copy in copies:
        copy.wait()
    x_copy.start()
    if by_rows is not None:
        for n in range(by_rows.shape[0] // 128):
            by_rows[n * 128 : n * 128 + 128, :] = w_ref[:, n * 128 : n * 128 + 128].T
        w_ref = by_rows
    noise_all(w_ref, out_ref, rank, seed, by_rows is not None)
    x_copy.wait()
    for n in range(2):
        part = slice(n * rows // 2, n * rows // 2 + rows // 2)
        own_ref[part, :] = dot(x_ref[part, :], out_ref[...]).astype(BF)


def perturb_same(place, seeds_ref, w0_ref, w1_ref, x_from, out_ref, own_ref, w_ref, x_ref, sems):
    for core, w_from in ((0, w0_ref), (1, w1_ref)):

        @pl.when(place[0] == core)
        def _(core=core, w_from=w_from):
            perturb_one(w_from, x_from, seeds_ref[1 + core], place[3], out_ref, own_ref, w_ref, x_ref, sems, None)


def perturb_mixed(place, seeds_ref, w0_ref, w1_ref, x0_from, x1_from, out_ref, own_ref, w_ref, x_ref, sems, wide_ref):
    @pl.when(place[0] == 0)
    def _():
        perturb_one(w0_ref, x0_from, seeds_ref[0], place[3], out_ref, own_ref, w_ref, x_ref, sems, None)

    @pl.when(place[0] == 1)
    def _():
        perturb_one(w1_ref, x1_from, seeds_ref[3], place[3], out_ref, own_ref, wide_ref, x_ref, sems, w_ref)


def perturb(run, kernel, seeds, w0, w1, activations, mib):
    rows, cols = w0.shape
    tokens = activations[0].shape
    wide = [pltpu.VMEM(w1.shape, BF)] if w1.shape != w0.shape else []
    return run.call(
        kernel, [shape(rows, cols, BF), shape(tokens[0], cols, BF)], [seeds, w0, w1, *activations],
        [SMEM] + [HBM] * (2 + len(activations)),
        [pltpu.VMEM((rows, cols), BF), pltpu.VMEM(tokens, BF), pltpu.SemaphoreType.DMA((9,))] + wide, 7.0, mib)


def capped(k, q):
    t = jnp.tanh(dot_bt(k, q) * (SCALE / CAP))
    return t, jnp.exp(CAP * t)


def levels_kernel(place, own_ref, other_ref, send_ref, near_ref, chip_ref, chip_next_ref):
    core = place[0]
    send_ref[...] = halve(halve(own_ref[...]))
    near_ref[...] = halve(halve(other_ref[...]))
    chip_ref[rows_at(core * 64, 64), :] = halve(send_ref[...])
    chip_ref[rows_at(64 - core * 64, 64), :] = halve(near_ref[...])
    chip_next_ref[...] = halve(chip_ref[...])


def local_forward(place, mine_ref, their_ref, w2_mine_ref, w2_their_ref,
                  q_ref, ga_ref, kl_ref, vl_ref, num_ref, sum_ref):
    for core, (first, second, q_in, ga_in) in (
        (0, (kl_ref, vl_ref, w2_mine_ref, w2_their_ref)),
        (1, (vl_ref, kl_ref, w2_their_ref, w2_mine_ref)),
    ):

        @pl.when(place[0] == core)
        def _(first=first, second=second, q_in=q_in, ga_in=ga_in):
            q_ref[...] = q_in[...]
            ga_ref[...] = ga_in[...]
            for into, rows_in in ((first, mine_ref), (second, their_ref)):
                upper = halve(rows_in[...])
                into[:256, :] = rows_in[:256, :]
                into[256:384, :] = upper[128:, :]
                into[384:640, :] = rows_in[256:, :]
                into[640:, :] = upper[:128, :]

    for h in range(q_ref.shape[1] // DH):
        hs = slice(h * DH, h * DH + DH)
        for pair in range(2):
            rows, keys = slice(pair * 256, pair * 256 + 256), slice(pair * 384, pair * 384 + 384)
            _, e = capped(kl_ref[keys, hs], q_ref[rows, hs])
            w = jnp.concatenate([e[:256], 2.0 * e[256:]], axis=0)
            num_ref[hs, rows] = dot_at(vl_ref[keys, hs], w.astype(BF))
            sum_ref[h : h + 1, rows] = jnp.sum(w, axis=0, keepdims=True)


def far_kernel(place, q_ref, near_mine, near_their, mine_a, mine_b, their_a, their_b, num_ref, sum_ref, ga_ref,
               att_ref, att_keep, att_give, inv_ref, rd_ref, dq_ref, keep_ref, send_ref, kf, vf, dkf, dvf):
    core = place[0]
    for is_core, (mine, their) in ((0, (kf, vf)), (1, (vf, kf))):

        @pl.when(core == is_core)
        def _(mine=mine, their=their):
            for into, near, first, second in ((mine, near_mine, mine_a, mine_b), (their, near_their, their_a, their_b)):
                into[:128, :] = near[...]
                into[128:384, :] = first[...]
                into[384:, :] = second[...]

    for h in range(q_ref.shape[1] // DH):
        hs = slice(h * DH, h * DH + DH)
        q, k, v, ga = q_ref[:, hs], kf[:, hs], vf[:, hs], ga_ref[:, hs]
        t, e = capped(k, q)
        w = jnp.concatenate([e[n * 128 : n * 128 + 128] * float(4 << n) for n in range(5)], axis=0)
        inv = 1.0 / (sum_ref[h : h + 1, :] + jnp.sum(w, axis=0, keepdims=True))
        att = ((num_ref[hs, :] + dot_at(v, w.astype(BF))) * inv).T.astype(BF)
        att_ref[:, hs] = att
        rd = jnp.sum((ga.astype(F32) * att.astype(F32)).T, axis=0, keepdims=True)
        inv_ref[h : h + 1, :] = inv
        rd_ref[h : h + 1, :] = rd
        p = w * inv
        dvf[:, hs] = dot(p.astype(BF), ga)
        g = (p * (dot_bt(v, ga) - rd) * (1.0 - t * t)).astype(BF)
        dq_ref[hs, :] = dot_at(k, g)
        dkf[:, hs] = dot(g, q) * SCALE

    half = att_keep.shape[1]
    att_keep[...] = att_ref[:, rows_at(core * half, half)]
    att_give[...] = att_ref[:, rows_at(half - core * half, half)]
    send_ref[:128, :] = dkf[:128, :].astype(BF)
    send_ref[128:256, :] = dvf[:128, :].astype(BF)
    for is_core, (keep, give) in ((0, (dkf, dvf)), (1, (dvf, dkf))):

        @pl.when(core == is_core)
        def _(keep=keep, give=give):
            keep_ref[...] = keep[128:, :]
            send_ref[256:, :] = give[128:, :].astype(BF)


def local_backward(place, q_ref, kl_ref, vl_ref, inv_ref, rd_ref, ga_ref, dqf_ref,
                   dq_ref, dq_keep, dq_give, dkv_ref, d1_ref):
    width = q_ref.shape[1]
    for h in range(width // DH):
        hs = slice(h * DH, h * DH + DH)
        hv = slice(width + h * DH, width + h * DH + DH)
        for pair in range(2):
            rows, keys = slice(pair * 256, pair * 256 + 256), slice(pair * 384, pair * 384 + 384)
            other = slice((1 - pair) * 128, (1 - pair) * 128 + 128)
            q, ga, k, v = q_ref[rows, hs], ga_ref[rows, hs], kl_ref[keys, hs], vl_ref[keys, hs]
            t, e = capped(k, q)
            inv = inv_ref[h : h + 1, rows]
            p = jnp.concatenate([e[:256] * inv, e[256:] * (2.0 * inv)], axis=0)
            dv = dot(p.astype(BF), ga)
            g = (p * (dot_bt(v, ga) - rd_ref[h : h + 1, rows]) * (1.0 - t * t)).astype(BF)
            dq_ref[rows, hs] = ((dqf_ref[hs, rows] + dot_at(k, g)) * SCALE).T.astype(BF)
            dk = dot(g, q) * SCALE
            dkv_ref[rows, hs] = dk[:256]
            dkv_ref[rows, hv] = dv[:256]
            d1_ref[other, hs] = dk[256:]
            d1_ref[other, hv] = dv[256:]
    dkv_ref[...] += expand(d1_ref[...])
    core, half = place[0], dq_keep.shape[1]
    dq_keep[...] = dq_ref[:, rows_at(core * half, half)]
    dq_give[...] = dq_ref[:, rows_at(half - core * half, half)]


def out_x(place, own_ref, one_ref, two_ref, three_ref, sets_ref, row_ref, row_next_ref):
    x = place[1]
    odd = x & 1
    sets_ref[:128, :] = one_ref[...]
    sets_ref[rows_at(128 + 64 * odd, 64), :] = two_ref[...]
    sets_ref[rows_at(192 - 64 * odd, 64), :] = three_ref[...]
    for apart, part in ((0, own_ref[...]), (1, halve(one_ref[...])), (2, two_ref[...]), (3, three_ref[...])):
        row_ref[rows_at(32 * (x ^ apart), 32), :] = halve(part)
    row_next_ref[...] = halve(row_ref[...])


def out_z(place, one_ref, two_ref, three_ref, sets_ref):
    odd = place[2] & 1
    sets_ref[:128, :] = one_ref[...]
    sets_ref[rows_at(128 + 64 * odd, 64), :] = two_ref[...]
    sets_ref[rows_at(192 - 64 * odd, 64), :] = three_ref[...]


def back_core(place, keep_ref, got_ref, near_ref, one_ref, two_ref, three_ref):
    odd = place[2] & 1
    near_ref[...] = keep_ref[:256, :] + got_ref[256:512, :].astype(F32)
    one_ref[...] = (keep_ref[256:384, :] + got_ref[512:640, :].astype(F32)).astype(BF)
    for into, first in ((two_ref, odd), (three_ref, 1 - odd)):
        kept = keep_ref[rows_at(384 + 64 * first, 64), :]
        into[...] = (kept + got_ref[rows_at(640 + 64 * first, 64), :].astype(F32)).astype(BF)


def back_z(place, near_ref, one_ref, two_ref, three_ref, own_out, one_out, two_out, three_out, row_ref):
    x = place[1]
    odd = x & 1
    row_ref[...] = one_ref[...].astype(F32) + expand(two_ref[...].astype(F32) + three_ref[...].astype(F32))

    def part(apart):
        return row_ref[rows_at(32 * (x ^ apart), 32), :]

    own_out[...] = part(0)
    one_out[...] = (near_ref[:128, :] + expand(part(1), 2)).astype(BF)
    for into, apart, first in ((two_out, 2, odd), (three_out, 3, 1 - odd)):
        into[...] = (near_ref[rows_at(128 + 64 * first, 64), :] + expand(part(apart))).astype(BF)


def back_x(place, own_ref, one_ref, two_ref, three_ref, keep_ref, send_ref, chip_ref):
    core = place[0]
    pair = two_ref[...].astype(F32) + three_ref[...].astype(F32) + expand(own_ref[...])
    chip_ref[...] = one_ref[...].astype(F32) + expand(pair)
    keep_ref[...] = chip_ref[rows_at(64 * core, 64), :]
    send_ref[...] = chip_ref[rows_at(64 - 64 * core, 64), :].astype(BF)


def back_last(place, keep3_ref, got3_ref, got_ref, dkv_ref, mine_ref, their_ref, keep_ref, give_ref):
    width = keep3_ref.shape[1]
    half = width // 2
    for core in range(2):

        @pl.when(place[0] == core)
        def _(core=core):
            for n in range(2):
                upper = keep3_ref[...] if n == core else got3_ref[...].astype(F32)
                level = got_ref[n * 128 : n * 128 + 128, :].astype(F32) + expand(upper)
                done = (dkv_ref[:, n * width : n * width + width] + expand(level, 2)).astype(BF)
                (mine_ref if n == core else their_ref)[...] = done
                keep_ref[:, n * half : n * half + half] = done[:, core * half : core * half + half]
                give_ref[:, n * half : n * half + half] = done[:, half - core * half : width - core * half]


def part_shapes(*dims):
    return [jax.ShapeDtypeStruct(dims, F32)] + [jax.ShapeDtypeStruct(dims, BF)] * 3


def send_parts(parts, axis):
    own, one, two, three = parts
    return own, shift(one, axis, 1), shift(two, axis, 2), shift(three, axis, -1)


def total(own, one, two, three):
    return own + one.astype(F32) + two.astype(F32) + three.astype(F32)


def ring_shapes(*dims):
    half = (*dims[:-2], dims[-2] // 2, dims[-1])
    full = [jax.ShapeDtypeStruct(dims, BF)] * 2
    return [jax.ShapeDtypeStruct(half, BF)] * 2 + full + [jax.ShapeDtypeStruct(dims, F32)]


def ring_start(parts, axis):
    two_up, two_down, one, three, own = parts
    return shift(two_up, axis, 1), shift(two_down, axis, -1), one, three, own


def ring_middle(place, one_ref, three_ref, up_ref, down_ref, up_out, down_out):
    half = up_ref.shape[-2]
    low, high = (..., slice(0, half), slice(None)), (..., slice(half, None), slice(None))
    up_out[low] = (one_ref[low].astype(F32) + up_ref[...].astype(F32)).astype(BF)
    up_out[high] = one_ref[high]
    down_out[low] = three_ref[low]
    down_out[high] = (three_ref[high].astype(F32) + down_ref[...].astype(F32)).astype(BF)


def ring_mid(run, ring):
    up, down, one, three, own = ring
    return *run(ring_middle, [jax.ShapeDtypeStruct(one.shape, BF)] * 2, [one, three, up, down]), own


def ring_go_on(ring, axis):
    up, down, own = ring
    return own, shift(up, axis, 1), shift(down, axis, -1)


def ring_total(own, up, down):
    return own + up.astype(F32) + down.astype(F32)


def ring_end(place, own_ref, up_ref, down_ref, out_ref):
    out_ref[...] = ring_total(own_ref[...], up_ref[...], down_ref[...]).astype(BF)


def ring_parts(rank, outs):
    return ((rank + 2) & 3, None), ((rank + 1) & 3, outs[2]), ((rank + 3) & 3, outs[3]), (rank, outs[4])


def write_ring(rank, width, product, outs):
    for whose, into in ring_parts(rank, outs):
        part = product(rows_at(whose * width, width))
        if into is None:
            rows = part.shape[0] // 2
            outs[0][...] = part[:rows].astype(BF)
            outs[1][...] = part[rows:].astype(BF)
        else:
            into[...] = part.astype(into.dtype)


def attended_parts(place, att_ref, w2_mine, w2_their, *outs):
    for core, w_ref in ((0, w2_their), (1, w2_mine)):

        @pl.when(place[0] == core)
        def _(w_ref=w_ref):
            write_ring(place[3], att_ref.shape[1], lambda rows: dot_bt(att_ref[...], w_ref[rows, :]), outs)


def input_parts(place, dq_ref, mine_ref, their_ref, w1_mine, w1_their, w2_mine, w2_their, *outs):
    for core, wq_ref in ((0, w2_mine), (1, w2_their)):

        @pl.when(place[0] == core)
        def _(wq_ref=wq_ref):
            def product(rows):
                terms = dot_bt(dq_ref[...], wq_ref[rows, :]) + dot_bt(mine_ref[...], w1_mine[rows, :])
                return terms + dot_bt(their_ref[...], w1_their[rows, :])

            write_ring(place[3], dq_ref.shape[1], product, outs)


def gradient_blocks(lhs, lhs_other, keep, got, cols):
    grads = jnp.concatenate([keep[...].T, got[...].T], axis=1)
    rows = [jnp.concatenate([lhs[:, c], lhs_other[:, c]], axis=0) for c in cols]
    return dot(grads, jnp.concatenate(rows, axis=1))


def early_terms(place, cot, cot_other, att_keep, att_got, tok, tok_other, dq_keep, dq_got, *outs):
    half = att_keep.shape[1]
    for n, sources in enumerate(((cot, cot_other, att_keep, att_got), (tok, tok_other, dq_keep, dq_got))):
        for whose, into in ring_parts(place[1], outs):
            at = n * half
            if into is None:
                into, at = outs[n], 0
            for pair in range(2):
                cols = [rows_at((2 * pair + m) * 512 + whose * 128, 128) for m in range(2)]
                part = gradient_blocks(*sources, cols).astype(into.dtype)
                for m in range(2):
                    into[2 * pair + m, at : at + half, :] = part[:, m * 128 : m * 128 + 128]


def late_terms(place, tok, tok_other, keep, got, *outs):
    half = outs[0].shape[1]
    for whose, into in ring_parts(place[2], outs):
        for pair in range(2):
            part = gradient_blocks(tok, tok_other, keep, got, [rows_at(whose * 512 + pair * 256, 256)])
            for n in range(2):
                block = part[:, n * 128 : n * 128 + 128]
                if into is None:
                    outs[0][2 * pair + n] = block[:half].astype(BF)
                    outs[1][2 * pair + n] = block[half:].astype(BF)
                else:
                    into[2 * pair + n] = block.astype(into.dtype)


def early_turn(place, *refs):
    turn(place[2], *refs)


def late_turn(place, *refs):
    turn(place[1], *refs)


def turn(at, own_ref, up_ref, down_ref, *outs):
    for by, into in enumerate(outs):
        n = (at + by) & 3
        into[...] = ring_total(own_ref[n], up_ref[n], down_ref[n]).astype(into.dtype)


def chip_sums(place, *refs):
    early, late, (keep_ref, give_ref, turned) = refs[:4], refs[4:8], refs[8:]
    width = early[0].shape[0]
    for n, parts in enumerate((early, late)):
        turned[:, n * width : n * width + width] = total(*(r[...] for r in parts)).T
    keep_ref[...] = turned[rows_at(place[0] * 64, 64), :]
    give_ref[...] = turned[rows_at(64 - place[0] * 64, 64), :]


def last_parts(place, keep_ref, got_ref, *outs):
    half = outs[0].shape[1] // 2
    for core in range(2):

        @pl.when(place[0] == core)
        def _(core=core):
            for from_ref, side in ((keep_ref, core), (got_ref, 1 - core)):
                for n, into in enumerate(outs):
                    into[:, side * half : side * half + half] = from_ref[:, n * half : n * half + half]


def swap(rows, axis, apart):
    return lax.ppermute(rows, axis, [(i, i ^ apart) for i in range(lax.axis_size(axis))])


def shift(rows, axis, by):
    n = lax.axis_size(axis)
    return lax.ppermute(rows, axis, [(i, (i + by) % n) for i in range(n)])


def body(tokens, cotangent, w_query, w_key, w_value, w_out, seeds):
    run = Chain()
    core = lax.axis_index("core")
    rows = tokens.shape[0]
    width = w_query.shape[1]
    square, stats = shape(rows, width, BF), shape(width // DH, rows, F32)
    half_cols, turned = shape(rows, width // 2, BF), shape(width, rows, F32)
    part128, part64 = shape(128, width, BF), shape(64, width, BF)

    tok_other, cot_other = swap(tokens, "core", 1), swap(cotangent, "core", 1)

    w1, mine0 = perturb(run, perturb_same, seeds, w_key, w_value, [tokens], 56)
    give0 = dot(tok_other, w1).astype(BF)
    their0 = swap(give0, "core", 1)
    w1_other = swap(w1, "core", 1)
    cot_other = run.hold(cot_other)[0]
    level2, near_mine, chip, chip_next = run(levels_kernel, [part128] * 3 + [part64], [mine0, give0])
    x1, x2, x3 = swap(chip, "x", 1), swap(chip_next, "x", 2), swap(chip_next, "x", 3)
    near_their = swap(level2, "core", 1)
    their0, near_their, w1_other = run.hold(their0, near_their, w1_other)

    w2, mine2 = perturb(run, perturb_mixed, seeds, w_query, w_out, [tokens, cotangent], 56)
    mine_a, row, row_next = run(out_x, [shape(256, width, BF), part128, part64], [chip_next, x1, x2, x3])
    z1, z2, z3 = swap(row, "z", 1), swap(row_next, "z", 2), swap(row_next, "z", 3)
    their_a = swap(mine_a, "core", 1)
    w2 = run.hold(w2)[0]
    give2 = dot(jnp.where(core == 0, tok_other, cot_other), w2).astype(BF)
    their2 = swap(give2, "core", 1)
    their_a, their2, w2 = run.hold(their_a, their2, w2)
    w2_other = swap(w2, "core", 1)

    queries, grad_att, kl, vl, num, total = run(
        local_forward, [square] * 2 + [shape(768, width, BF)] * 2 + [turned, stats], [mine0, their0, mine2, their2], us=3.0)
    mine_b = run(out_z, [shape(256, width, BF)], [z1, z2, z3])[0]
    their_b = swap(mine_b, "core", 1)
    att, att_keep, att_give, inv, rd, dq_far, keep, send = run(
        far_kernel,
        [square] + [half_cols] * 2 + [stats] * 2 + [turned, shape(512, width, F32), shape(768, width, BF)],
        [queries, near_mine, near_their, mine_a, mine_b, their_a, their_b, num, total, grad_att],
        [pltpu.VMEM((640, width), BF)] * 2 + [pltpu.VMEM((640, width), F32)] * 2, us=6.0)
    got, att_got = swap(send, "core", 1), swap(att_give, "core", 1)

    att_ring = run(attended_parts, ring_shapes(rows, width), [att, w2, w2_other], us=2.0)
    got, att_got = run.hold(got, att_got)
    near, b1, b2, b3 = run(back_core, [shape(256, width, F32), part128, part64, part64], [keep, got])
    b1, b2, b3 = swap(b1, "z", 1), swap(b2, "z", 2), swap(b3, "z", 3)
    att_ring = ring_start(att_ring, "head")
    dq, dq_keep, dq_give, dkv_local = run(
        local_backward, [square, half_cols, half_cols, shape(rows, 2 * width, F32)],
        [queries, kl, vl, inv, rd, grad_att, dq_far], [pltpu.VMEM((256, 2 * width), F32)], us=4.0)
    own, c1, c2, c3 = run(
        back_z, [shape(32, width, F32), part128, part64, part64], [near, b1, b2, b3], [pltpu.VMEM((128, width), F32)])
    c1, c2, c3 = swap(c1, "x", 1), swap(c2, "x", 2), swap(c3, "x", 3)
    dq_give = run.hold(dq_give)[0]
    dq_got = swap(dq_give, "core", 1)
    att_ring = ring_mid(run, att_ring)
    early = run(
        early_terms, ring_shapes(4, width, 128),
        [cotangent, cot_other, att_keep, att_got, tokens, tok_other, dq_keep, dq_got], us=5.0)
    early = ring_start(early, "x")
    keep3, send3 = run(back_x, [shape(64, width, F32), part64], [own, c1, c2, c3], [pltpu.VMEM((128, width), F32)])
    got3 = swap(send3, "core", 1)
    att_ring = ring_go_on(run.hold(*att_ring), "head")
    dkv_mine, dkv_their, dkv_keep, dkv_give = run(back_last, [square] * 4, [keep3, got3, got, dkv_local])
    dkv_got = swap(dkv_give, "core", 1)
    late = run(late_terms, ring_shapes(4, width, 128), [tokens, tok_other, dkv_keep, dkv_got], us=3.0)
    late = ring_start(late, "z")
    early = ring_go_on(ring_mid(run, early), "x")
    in_ring = run(input_parts, ring_shapes(rows, width),
                  [dq, dkv_mine, dkv_their, w1, w1_other, w2, w2_other], us=5.0)
    late = ring_go_on(ring_mid(run, late), "z")
    attended = run(ring_end, [square], att_ring)[0]
    in_ring = ring_start(run.hold(*in_ring), "head")
    early = send_parts(run(early_turn, part_shapes(width, 128), early), "z")
    in_ring = ring_go_on(ring_mid(run, in_ring), "head")
    late = send_parts(run(late_turn, part_shapes(width, 128), late), "x")
    grad_tokens = run(ring_end, [square], in_ring)[0]
    keep, give = run(chip_sums, [shape(64, 2 * width, F32)] * 2, [*early, *late], [pltpu.VMEM((128, 2 * width), F32)])
    grad_w_out, grad_w_query, grad_w_key, grad_w_value = run(
        last_parts, [shape(64, width, F32)] * 4, [keep, swap(give, "core", 1)])
    return (attended, grad_tokens, grad_w_query, grad_w_key, grad_w_value, grad_w_out.T)


def solution(mesh):
    fine = Mesh(mesh.devices.reshape(4, 4, 2, 4), SEQ + ("head",))
    in_specs = (
        P(SEQ, None),
        P(SEQ, None),
        P(None, "head"),
        P(None, "head"),
        P(None, "head"),
        P("head", None),
        P(),
    )
    out_specs = (P(SEQ, "head"),) * 5 + (P("head", SEQ),)
    return jax.shard_map(body, mesh=fine, in_specs=in_specs, out_specs=out_specs, check_vma=False)
```

```python
import math

import jax
import jax.numpy as jnp
from jax import lax
from jax.experimental import pallas as pl
from jax.experimental.pallas import tpu as pltpu
from jax.sharding import Mesh, PartitionSpec as P

DH = 128
LEAF = 128
PRIME = 32749
CAP = 6.0
HALF_NOISE = 0.5
SCALE = 1.0 / math.sqrt(DH)
BF = jnp.bfloat16
F32 = jnp.float32
SEQ = ("z", "x", "core")
VMEM = pl.BlockSpec(memory_space=pltpu.VMEM)
SMEM = pl.BlockSpec(memory_space=pltpu.SMEM)
HBM = pl.BlockSpec(memory_space=pltpu.HBM)
ANY = pl.BlockSpec(memory_space=pl.ANY)


def params(mib=24):
    return pltpu.CompilerParams(vmem_limit_bytes=mib << 20)


class Chain:
    def __init__(self):
        self.tick = None

    def call(self, kernel, outs, args, specs, scratch, us, mib=24, aliases={}, out_specs=None):
        first, used = self.tick is None, len(args)

        def run(*refs):
            ins, tick_in, rest = refs[:used], refs[used : used + 1 - first], refs[used + 1 - first :]
            rest[0][...] = jnp.zeros((1, 128), F32) if first else tick_in[0][...]
            kernel(here(), *ins, *rest[1:])

        ticks = [] if first else [self.tick]
        self.tick, *results = pl.pallas_call(
            run,
            out_shape=[shape(1, 128, F32), *outs],
            in_specs=specs + [VMEM] * len(ticks),
            out_specs=[VMEM] + (out_specs or [ANY if n in aliases else VMEM for n in range(len(outs))]),
            scratch_shapes=list(scratch),
            name=kernel.__name__,
            input_output_aliases={n: 1 + n for n in aliases},
            cost_estimate=pl.CostEstimate(flops=int(us * 1e9), bytes_accessed=1, transcendentals=0),
            compiler_params=params(mib),
        )(*args, *ticks)
        return results

    def __call__(self, kernel, outs, args, scratch=(), us=1.0):
        return self.call(kernel, outs, args, [VMEM] * len(args), scratch, us)

    def hold(self, *arrays):
        return self.call(
            wait_here, [jax.ShapeDtypeStruct(a.shape, a.dtype) for a in arrays], arrays, [ANY] * len(arrays), (), 0.1,
            aliases=range(len(arrays)))


def wait_here(place, *refs):
    pass


def here():
    return [lax.axis_index(name) for name in ("core", "x", "z", "head")]


def shape(rows, cols, dtype):
    return jax.ShapeDtypeStruct((rows, cols), dtype)


def dot(a, b):
    return jnp.dot(a, b, preferred_element_type=F32)


def dot_bt(a, b):
    return lax.dot_general(a, b, (((1,), (1,)), ((), ())), preferred_element_type=F32)


def dot_at(a, b):
    return lax.dot_general(a, b, (((0,), (0,)), ((), ())), preferred_element_type=F32)


def rows_at(start, count):
    return pl.ds(pl.multiple_of(start, count), count)


def halve(rows_in):
    rows = rows_in.shape[0]
    out_row = lax.broadcasted_iota(jnp.int32, (rows // 2, rows), 0)
    in_row = lax.broadcasted_iota(jnp.int32, (rows // 2, rows), 1)
    average = jnp.where(lax.shift_right_logical(in_row, 1) == out_row, 0.5, 0.0).astype(BF)
    return dot(average, rows_in).astype(BF)


def expand(rows_in, shift=1):
    rows, times = rows_in.shape[0], 1 << shift
    out_row = lax.broadcasted_iota(jnp.int32, (rows * times, rows), 0)
    in_row = lax.broadcasted_iota(jnp.int32, (rows * times, rows), 1)
    spread = jnp.where(lax.shift_right_logical(out_row, shift) == in_row, 1.0 / times, 0.0).astype(BF)
    high = rows_in.astype(BF)
    low = (rows_in - high.astype(F32)).astype(BF)
    return dot(spread, high) + dot(spread, low)


def fold(value):
    for _ in range(2):
        value = lax.shift_right_logical(value, 15) * 19 + (value & 32767)
    return value


def below_prime(value):
    return jnp.where(value >= PRIME, value - PRIME, value)


def hash_of(row_part, col_part, row_ids, col_ids):
    h = row_part + col_part
    f = h.astype(F32)
    quotient = (f * (f * (1.0 / PRIME))).astype(jnp.int32)
    h = h * h - quotient * PRIME + col_ids
    return below_prime(fold(h * h + row_ids)).astype(F32)


def add_squares(w_ref, start, rows, acc):
    def add(i, acc):
        w = w_ref[rows_at(start + i * 64, 64), :].astype(F32)
        return acc + jnp.sum((w * w).reshape(8, 8, w.shape[1]), axis=0)

    return lax.fori_loop(0, rows // 64, add, acc)


def noise_all(w_ref, out_ref, squares, rank, seed, lanes_are_rows, written):
    rows, cols = w_ref.shape
    chunk = 64
    mult, lane_mult = (10007, 7919) if lanes_are_rows else (7919, 10007)
    own_ids = lax.broadcasted_iota(jnp.int32, (1, cols), 1) + rank * cols
    own_part = below_prime(below_prime(fold(own_ids * lane_mult)) + below_prime(fold(seed * 31337)))
    mean = jnp.sum(squares, axis=0, keepdims=True) * (1.0 / rows)
    amp = HALF_NOISE * jnp.sqrt(mean + 1e-06)
    slope = amp * (2.0 / (PRIME - 1))

    def step(i, carry):
        ids, part = carry
        for lane in range(cols // 128):
            here = slice(lane * 128, lane * 128 + 128)
            lane_ids, lane_part = own_ids[:, here], own_part[:, here]
            if lanes_are_rows:
                hashed = hash_of(lane_part, part, lane_ids, ids)
            else:
                hashed = hash_of(part, lane_part, ids, lane_ids)
            w = w_ref[rows_at(i * chunk, chunk), here].astype(F32)
            out_ref[rows_at(i * chunk, chunk), here] = ((w - amp[:, here]) + slope[:, here] * hashed).astype(BF)
        return ids + chunk, below_prime(part + chunk * mult % PRIME)

    ids = lax.broadcasted_iota(jnp.int32, (chunk, 128), 0)
    carry = (ids, ids * mult % PRIME)
    steps = rows // chunk // 4
    for n in range(4):
        carry = lax.fori_loop(n * steps, n * steps + steps, step, carry, unroll=2)
        written(n)


def perturb_one(w_from, x_from, seed, rank, out_hbm, own_ref, w_ref, x_ref, new_ref, sems, turned):
    rows, cols = new_ref.shape
    piece, quarter = w_ref.shape[0] // 8, rows // 4
    x_copy = pltpu.make_async_copy(x_from, x_ref, sems.at[8])
    ins = [
        pltpu.make_async_copy(w_from.at[pl.ds(n * piece, piece), :], w_ref.at[pl.ds(n * piece, piece), :], sems.at[n])
        for n in range(8)
    ]
    outs = [
        pltpu.make_async_copy(
            new_ref.at[pl.ds(n * quarter, quarter), :], out_hbm.at[pl.ds(n * quarter, quarter), :], sems.at[9 + n])
        for n in range(4)
    ]
    for copy in ins:
        copy.start()
    squares = jnp.zeros((8, cols), F32)
    for n, copy in enumerate(ins):
        copy.wait()
        if turned is None:
            squares = add_squares(w_ref, n * piece, piece, squares)
    x_copy.start()
    if turned is not None:
        for n in range(rows // 128):
            turned[n * 128 : n * 128 + 128, :] = w_ref[:, n * 128 : n * 128 + 128].T
        squares = add_squares(turned, 0, rows, squares)
        w_ref = turned
    noise_all(w_ref, new_ref, squares, rank, seed, turned is not None, lambda n: outs[n].start())
    x_copy.wait()
    for n in range(2):
        part = slice(n * x_ref.shape[0] // 2, (n + 1) * x_ref.shape[0] // 2)
        own_ref[part, :] = dot(x_ref[part, :], new_ref[...]).astype(BF)
    for copy in outs:
        copy.wait()


def perturb_same(place, seeds_ref, w0_ref, w1_ref, x_from, out_hbm, own_ref, w_ref, x_ref, new_ref, sems):
    for core, w_from in ((0, w0_ref), (1, w1_ref)):

        @pl.when(place[0] == core)
        def _(core=core, w_from=w_from):
            perturb_one(w_from, x_from, seeds_ref[1 + core], place[3], out_hbm, own_ref, w_ref, x_ref, new_ref, sems, None)


def perturb_mixed(place, seeds_ref, w0_ref, w1_ref, x0_from, x1_from, out_hbm, own_ref, w_ref, x_ref, new_ref, sems, wide_ref):
    @pl.when(place[0] == 0)
    def _():
        perturb_one(w0_ref, x0_from, seeds_ref[0], place[3], out_hbm, own_ref, w_ref, x_ref, new_ref, sems, None)

    @pl.when(place[0] == 1)
    def _():
        perturb_one(w1_ref, x1_from, seeds_ref[3], place[3], out_hbm, own_ref, wide_ref, x_ref, new_ref, sems, w_ref)


def perturb(run, kernel, seeds, w0, w1, activations, mib):
    rows, cols = w0.shape
    tokens = activations[0].shape
    wide = [pltpu.VMEM(w1.shape, BF)] if w1.shape != w0.shape else []
    return run.call(
        kernel, [shape(rows, cols, BF), shape(tokens[0], cols, BF)], [seeds, w0, w1, *activations],
        [SMEM] + [HBM] * (2 + len(activations)),
        [pltpu.VMEM((rows, cols), BF), pltpu.VMEM(tokens, BF), pltpu.VMEM((rows, cols), BF), pltpu.SemaphoreType.DMA((13,))]
        + wide, 7.0, mib, out_specs=[HBM, VMEM])


def capped(k, q):
    t = jnp.tanh(dot_bt(k, q) * (SCALE / CAP))
    return t, jnp.exp(CAP * t)


def levels_kernel(place, own_ref, other_ref, send_ref, near_ref, chip_ref, chip_next_ref):
    core = place[0]
    send_ref[...] = halve(halve(own_ref[...]))
    near_ref[...] = halve(halve(other_ref[...]))
    chip_ref[rows_at(core * 64, 64), :] = halve(send_ref[...])
    chip_ref[rows_at(64 - core * 64, 64), :] = halve(near_ref[...])
    chip_next_ref[...] = halve(chip_ref[...])


def local_forward(place, mine_ref, their_ref, w2_mine_ref, w2_their_ref,
                  q_ref, ga_ref, kl_ref, vl_ref, num_ref, sum_ref):
    for core, (first, second, q_in, ga_in) in (
        (0, (kl_ref, vl_ref, w2_mine_ref, w2_their_ref)),
        (1, (vl_ref, kl_ref, w2_their_ref, w2_mine_ref)),
    ):

        @pl.when(place[0] == core)
        def _(first=first, second=second, q_in=q_in, ga_in=ga_in):
            q_ref[...] = q_in[...]
            ga_ref[...] = ga_in[...]
            for into, rows_in in ((first, mine_ref), (second, their_ref)):
                upper = halve(rows_in[...])
                into[:256, :] = rows_in[:256, :]
                into[256:384, :] = upper[128:, :]
                into[384:640, :] = rows_in[256:, :]
                into[640:, :] = upper[:128, :]

    for h in range(q_ref.shape[1] // DH):
        hs = slice(h * DH, h * DH + DH)
        for pair in range(2):
            rows, keys = slice(pair * 256, pair * 256 + 256), slice(pair * 384, pair * 384 + 384)
            _, e = capped(kl_ref[keys, hs], q_ref[rows, hs])
            w = jnp.concatenate([e[:256], 2.0 * e[256:]], axis=0)
            num_ref[hs, rows] = dot_at(vl_ref[keys, hs], w.astype(BF))
            sum_ref[h : h + 1, rows] = jnp.sum(w, axis=0, keepdims=True)


def far_kernel(place, q_ref, near_mine, near_their, mine_a, mine_b, their_a, their_b, num_ref, sum_ref, ga_ref,
               att_ref, att_keep, att_give, inv_ref, rd_ref, dq_ref, keep_ref, send_ref, kf, vf, dkf, dvf):
    core = place[0]
    for is_core, (mine, their) in ((0, (kf, vf)), (1, (vf, kf))):

        @pl.when(core == is_core)
        def _(mine=mine, their=their):
            for into, near, first, second in ((mine, near_mine, mine_a, mine_b), (their, near_their, their_a, their_b)):
                into[:128, :] = near[...]
                into[128:384, :] = first[...]
                into[384:, :] = second[...]

    for h in range(q_ref.shape[1] // DH):
        hs = slice(h * DH, h * DH + DH)
        q, k, v, ga = q_ref[:, hs], kf[:, hs], vf[:, hs], ga_ref[:, hs]
        t, e = capped(k, q)
        w = jnp.concatenate([e[n * 128 : n * 128 + 128] * float(4 << n) for n in range(5)], axis=0)
        inv = 1.0 / (sum_ref[h : h + 1, :] + jnp.sum(w, axis=0, keepdims=True))
        att = ((num_ref[hs, :] + dot_at(v, w.astype(BF))) * inv).T.astype(BF)
        att_ref[:, hs] = att
        rd = jnp.sum((ga.astype(F32) * att.astype(F32)).T, axis=0, keepdims=True)
        inv_ref[h : h + 1, :] = inv
        rd_ref[h : h + 1, :] = rd
        p = w * inv
        dvf[:, hs] = dot(p.astype(BF), ga)
        g = (p * (dot_bt(v, ga) - rd) * (1.0 - t * t)).astype(BF)
        dq_ref[hs, :] = dot_at(k, g)
        dkf[:, hs] = dot(g, q) * SCALE

    half = att_keep.shape[1]
    att_keep[...] = att_ref[:, rows_at(core * half, half)]
    att_give[...] = att_ref[:, rows_at(half - core * half, half)]
    send_ref[:128, :] = dkf[:128, :].astype(BF)
    send_ref[128:256, :] = dvf[:128, :].astype(BF)
    for is_core, (keep, give) in ((0, (dkf, dvf)), (1, (dvf, dkf))):

        @pl.when(core == is_core)
        def _(keep=keep, give=give):
            keep_ref[...] = keep[128:, :]
            send_ref[256:, :] = give[128:, :].astype(BF)


def local_backward(place, q_ref, kl_ref, vl_ref, inv_ref, rd_ref, ga_ref, dqf_ref,
                   dq_ref, dq_keep, dq_give, dkv_ref, d1_ref):
    width = q_ref.shape[1]
    for h in range(width // DH):
        hs = slice(h * DH, h * DH + DH)
        hv = slice(width + h * DH, width + h * DH + DH)
        for pair in range(2):
            rows, keys = slice(pair * 256, pair * 256 + 256), slice(pair * 384, pair * 384 + 384)
            other = slice((1 - pair) * 128, (1 - pair) * 128 + 128)
            q, ga, k, v = q_ref[rows, hs], ga_ref[rows, hs], kl_ref[keys, hs], vl_ref[keys, hs]
            t, e = capped(k, q)
            inv = inv_ref[h : h + 1, rows]
            p = jnp.concatenate([e[:256] * inv, e[256:] * (2.0 * inv)], axis=0)
            dv = dot(p.astype(BF), ga)
            g = (p * (dot_bt(v, ga) - rd_ref[h : h + 1, rows]) * (1.0 - t * t)).astype(BF)
            dq_ref[rows, hs] = ((dqf_ref[hs, rows] + dot_at(k, g)) * SCALE).T.astype(BF)
            dk = dot(g, q) * SCALE
            dkv_ref[rows, hs] = dk[:256]
            dkv_ref[rows, hv] = dv[:256]
            d1_ref[other, hs] = dk[256:]
            d1_ref[other, hv] = dv[256:]
    dkv_ref[...] += expand(d1_ref[...])
    core, half = place[0], dq_keep.shape[1]
    dq_keep[...] = dq_ref[:, rows_at(core * half, half)]
    dq_give[...] = dq_ref[:, rows_at(half - core * half, half)]


def out_x(place, own_ref, one_ref, two_ref, three_ref, sets_ref, row_ref, row_next_ref):
    x = place[1]
    odd = x & 1
    sets_ref[:128, :] = one_ref[...]
    sets_ref[rows_at(128 + 64 * odd, 64), :] = two_ref[...]
    sets_ref[rows_at(192 - 64 * odd, 64), :] = three_ref[...]
    for apart, part in ((0, own_ref[...]), (1, halve(one_ref[...])), (2, two_ref[...]), (3, three_ref[...])):
        row_ref[rows_at(32 * (x ^ apart), 32), :] = halve(part)
    row_next_ref[...] = halve(row_ref[...])


def out_z(place, one_ref, two_ref, three_ref, sets_ref):
    odd = place[2] & 1
    sets_ref[:128, :] = one_ref[...]
    sets_ref[rows_at(128 + 64 * odd, 64), :] = two_ref[...]
    sets_ref[rows_at(192 - 64 * odd, 64), :] = three_ref[...]


def back_core(place, keep_ref, got_ref, near_ref, one_ref, two_ref, three_ref):
    odd = place[2] & 1
    near_ref[...] = keep_ref[:256, :] + got_ref[256:512, :].astype(F32)
    one_ref[...] = (keep_ref[256:384, :] + got_ref[512:640, :].astype(F32)).astype(BF)
    for into, first in ((two_ref, odd), (three_ref, 1 - odd)):
        kept = keep_ref[rows_at(384 + 64 * first, 64), :]
        into[...] = (kept + got_ref[rows_at(640 + 64 * first, 64), :].astype(F32)).astype(BF)


def back_z(place, near_ref, one_ref, two_ref, three_ref, own_out, one_out, two_out, three_out, row_ref):
    x = place[1]
    odd = x & 1
    row_ref[...] = one_ref[...].astype(F32) + expand(two_ref[...].astype(F32) + three_ref[...].astype(F32))

    def part(apart):
        return row_ref[rows_at(32 * (x ^ apart), 32), :]

    own_out[...] = part(0)
    one_out[...] = (near_ref[:128, :] + expand(part(1), 2)).astype(BF)
    for into, apart, first in ((two_out, 2, odd), (three_out, 3, 1 - odd)):
        into[...] = (near_ref[rows_at(128 + 64 * first, 64), :] + expand(part(apart))).astype(BF)


def back_x(place, own_ref, one_ref, two_ref, three_ref, keep_ref, send_ref, chip_ref):
    core = place[0]
    pair = two_ref[...].astype(F32) + three_ref[...].astype(F32) + expand(own_ref[...])
    chip_ref[...] = one_ref[...].astype(F32) + expand(pair)
    keep_ref[...] = chip_ref[rows_at(64 * core, 64), :]
    send_ref[...] = chip_ref[rows_at(64 - 64 * core, 64), :].astype(BF)


def back_last(place, keep3_ref, got3_ref, got_ref, dkv_ref, mine_ref, their_ref, keep_ref, give_ref):
    width = keep3_ref.shape[1]
    half = width // 2
    for core in range(2):

        @pl.when(place[0] == core)
        def _(core=core):
            for n in range(2):
                upper = keep3_ref[...] if n == core else got3_ref[...].astype(F32)
                level = got_ref[n * 128 : n * 128 + 128, :].astype(F32) + expand(upper)
                done = (dkv_ref[:, n * width : n * width + width] + expand(level, 2)).astype(BF)
                (mine_ref if n == core else their_ref)[...] = done
                keep_ref[:, n * half : n * half + half] = done[:, core * half : core * half + half]
                give_ref[:, n * half : n * half + half] = done[:, half - core * half : width - core * half]


def part_shapes(*dims):
    return [jax.ShapeDtypeStruct(dims, F32)] + [jax.ShapeDtypeStruct(dims, BF)] * 3


def send_parts(parts, axis):
    own, one, two, three = parts
    return own, shift(one, axis, 1), shift(two, axis, 2), shift(three, axis, -1)


def total(own, one, two, three):
    return own + one.astype(F32) + two.astype(F32) + three.astype(F32)


def ring_shapes(*dims):
    half = (*dims[:-2], dims[-2] // 2, dims[-1])
    full = [jax.ShapeDtypeStruct(dims, BF)] * 2
    return [jax.ShapeDtypeStruct(half, BF)] * 2 + full + [jax.ShapeDtypeStruct(dims, F32)]


def ring_start(parts, axis):
    two_up, two_down, one, three, own = parts
    return shift(two_up, axis, 1), shift(two_down, axis, -1), one, three, own


def ring_middle(place, one_ref, three_ref, up_ref, down_ref, up_out, down_out):
    half = up_ref.shape[-2]
    low, high = (..., slice(0, half), slice(None)), (..., slice(half, None), slice(None))
    up_out[low] = (one_ref[low].astype(F32) + up_ref[...].astype(F32)).astype(BF)
    up_out[high] = one_ref[high]
    down_out[low] = three_ref[low]
    down_out[high] = (three_ref[high].astype(F32) + down_ref[...].astype(F32)).astype(BF)


def ring_mid(run, ring):
    up, down, one, three, own = ring
    return *run(ring_middle, [jax.ShapeDtypeStruct(one.shape, BF)] * 2, [one, three, up, down]), own


def ring_go_on(ring, axis):
    up, down, own = ring
    return own, shift(up, axis, 1), shift(down, axis, -1)


def ring_total(own, up, down):
    return own + up.astype(F32) + down.astype(F32)


def ring_end(place, own_ref, up_ref, down_ref, out_ref):
    out_ref[...] = ring_total(own_ref[...], up_ref[...], down_ref[...]).astype(BF)


def ring_parts(rank, outs):
    return ((rank + 2) & 3, None), ((rank + 1) & 3, outs[2]), ((rank + 3) & 3, outs[3]), (rank, outs[4])


def write_ring(rank, width, product, outs):
    for whose, into in ring_parts(rank, outs):
        part = product(rows_at(whose * width, width))
        if into is None:
            rows = part.shape[0] // 2
            outs[0][...] = part[:rows].astype(BF)
            outs[1][...] = part[rows:].astype(BF)
        else:
            into[...] = part.astype(into.dtype)


def attended_parts(place, att_ref, w2_mine, w2_their, *outs):
    for core, w_ref in ((0, w2_their), (1, w2_mine)):

        @pl.when(place[0] == core)
        def _(w_ref=w_ref):
            write_ring(place[3], att_ref.shape[1], lambda rows: dot_bt(att_ref[...], w_ref[rows, :]), outs)


def input_parts(place, dq_ref, mine_ref, their_ref, w1_mine, w1_their, w2_mine, w2_their, *outs):
    for core, wq_ref in ((0, w2_mine), (1, w2_their)):

        @pl.when(place[0] == core)
        def _(wq_ref=wq_ref):
            def product(rows):
                terms = dot_bt(dq_ref[...], wq_ref[rows, :]) + dot_bt(mine_ref[...], w1_mine[rows, :])
                return terms + dot_bt(their_ref[...], w1_their[rows, :])

            write_ring(place[3], dq_ref.shape[1], product, outs)


def gradient_blocks(lhs, lhs_other, keep, got, cols):
    grads = jnp.concatenate([keep[...].T, got[...].T], axis=1)
    rows = [jnp.concatenate([lhs[:, c], lhs_other[:, c]], axis=0) for c in cols]
    return dot(grads, jnp.concatenate(rows, axis=1))


def early_terms(place, cot, cot_other, att_keep, att_got, tok, tok_other, dq_keep, dq_got, *outs):
    half = att_keep.shape[1]
    for n, sources in enumerate(((cot, cot_other, att_keep, att_got), (tok, tok_other, dq_keep, dq_got))):
        for whose, into in ring_parts(place[1], outs):
            at = n * half
            if into is None:
                into, at = outs[n], 0
            for pair in range(2):
                cols = [rows_at((2 * pair + m) * 512 + whose * 128, 128) for m in range(2)]
                part = gradient_blocks(*sources, cols).astype(into.dtype)
                for m in range(2):
                    into[2 * pair + m, at : at + half, :] = part[:, m * 128 : m * 128 + 128]


def late_terms(place, tok, tok_other, keep, got, *outs):
    half = outs[0].shape[1]
    for whose, into in ring_parts(place[2], outs):
        for pair in range(2):
            part = gradient_blocks(tok, tok_other, keep, got, [rows_at(whose * 512 + pair * 256, 256)])
            for n in range(2):
                block = part[:, n * 128 : n * 128 + 128]
                if into is None:
                    outs[0][2 * pair + n] = block[:half].astype(BF)
                    outs[1][2 * pair + n] = block[half:].astype(BF)
                else:
                    into[2 * pair + n] = block.astype(into.dtype)


def early_turn(place, *refs):
    turn(place[2], *refs)


def late_turn(place, *refs):
    turn(place[1], *refs)


def turn(at, own_ref, up_ref, down_ref, *outs):
    for by, into in enumerate(outs):
        n = (at + by) & 3
        into[...] = ring_total(own_ref[n], up_ref[n], down_ref[n]).astype(into.dtype)


def chip_sums(place, *refs):
    early, late, (keep_ref, give_ref, turned) = refs[:4], refs[4:8], refs[8:]
    width = early[0].shape[0]
    for n, parts in enumerate((early, late)):
        turned[:, n * width : n * width + width] = total(*(r[...] for r in parts)).T
    keep_ref[...] = turned[rows_at(place[0] * 64, 64), :]
    give_ref[...] = turned[rows_at(64 - place[0] * 64, 64), :]


def last_parts(place, keep_ref, got_ref, *outs):
    half = outs[0].shape[1] // 2
    for core in range(2):

        @pl.when(place[0] == core)
        def _(core=core):
            for from_ref, side in ((keep_ref, core), (got_ref, 1 - core)):
                for n, into in enumerate(outs):
                    into[:, side * half : side * half + half] = from_ref[:, n * half : n * half + half]


def swap(rows, axis, apart):
    return lax.ppermute(rows, axis, [(i, i ^ apart) for i in range(lax.axis_size(axis))])


def shift(rows, axis, by):
    n = lax.axis_size(axis)
    return lax.ppermute(rows, axis, [(i, (i + by) % n) for i in range(n)])


def body(tokens, cotangent, w_query, w_key, w_value, w_out, seeds):
    run = Chain()
    core = lax.axis_index("core")
    rows = tokens.shape[0]
    width = w_query.shape[1]
    square, stats = shape(rows, width, BF), shape(width // DH, rows, F32)
    half_cols, turned = shape(rows, width // 2, BF), shape(width, rows, F32)
    part128, part64 = shape(128, width, BF), shape(64, width, BF)

    tok_other, cot_other = swap(tokens, "core", 1), swap(cotangent, "core", 1)

    w1, mine0 = perturb(run, perturb_same, seeds, w_key, w_value, [tokens], 56)
    give0 = dot(tok_other, w1).astype(BF)
    their0 = swap(give0, "core", 1)
    w1_other = swap(w1, "core", 1)
    cot_other = run.hold(cot_other)[0]
    level2, near_mine, chip, chip_next = run(levels_kernel, [part128] * 3 + [part64], [mine0, give0])
    x1, x2, x3 = swap(chip, "x", 1), swap(chip_next, "x", 2), swap(chip_next, "x", 3)
    near_their = swap(level2, "core", 1)
    their0, near_their, w1_other = run.hold(their0, near_their, w1_other)

    w2, mine2 = perturb(run, perturb_mixed, seeds, w_query, w_out, [tokens, cotangent], 56)
    mine_a, row, row_next = run(out_x, [shape(256, width, BF), part128, part64], [chip_next, x1, x2, x3])
    z1, z2, z3 = swap(row, "z", 1), swap(row_next, "z", 2), swap(row_next, "z", 3)
    their_a = swap(mine_a, "core", 1)
    w2 = run.hold(w2)[0]
    give2 = dot(jnp.where(core == 0, tok_other, cot_other), w2).astype(BF)
    their2 = swap(give2, "core", 1)
    their_a, their2, w2 = run.hold(their_a, their2, w2)
    w2_other = swap(w2, "core", 1)

    queries, grad_att, kl, vl, num, total = run(
        local_forward, [square] * 2 + [shape(768, width, BF)] * 2 + [turned, stats], [mine0, their0, mine2, their2], us=3.0)
    mine_b = run(out_z, [shape(256, width, BF)], [z1, z2, z3])[0]
    their_b = swap(mine_b, "core", 1)
    att, att_keep, att_give, inv, rd, dq_far, keep, send = run(
        far_kernel,
        [square] + [half_cols] * 2 + [stats] * 2 + [turned, shape(512, width, F32), shape(768, width, BF)],
        [queries, near_mine, near_their, mine_a, mine_b, their_a, their_b, num, total, grad_att],
        [pltpu.VMEM((640, width), BF)] * 2 + [pltpu.VMEM((640, width), F32)] * 2, us=6.0)
    got, att_got = swap(send, "core", 1), swap(att_give, "core", 1)

    att_ring = run(attended_parts, ring_shapes(rows, width), [att, w2, w2_other], us=2.0)
    got, att_got = run.hold(got, att_got)
    near, b1, b2, b3 = run(back_core, [shape(256, width, F32), part128, part64, part64], [keep, got])
    b1, b2, b3 = swap(b1, "z", 1), swap(b2, "z", 2), swap(b3, "z", 3)
    att_ring = ring_start(att_ring, "head")
    dq, dq_keep, dq_give, dkv_local = run(
        local_backward, [square, half_cols, half_cols, shape(rows, 2 * width, F32)],
        [queries, kl, vl, inv, rd, grad_att, dq_far], [pltpu.VMEM((256, 2 * width), F32)], us=4.0)
    own, c1, c2, c3 = run(
        back_z, [shape(32, width, F32), part128, part64, part64], [near, b1, b2, b3], [pltpu.VMEM((128, width), F32)])
    c1, c2, c3 = swap(c1, "x", 1), swap(c2, "x", 2), swap(c3, "x", 3)
    dq_give = run.hold(dq_give)[0]
    dq_got = swap(dq_give, "core", 1)
    att_ring = ring_mid(run, att_ring)
    early = run(
        early_terms, ring_shapes(4, width, 128),
        [cotangent, cot_other, att_keep, att_got, tokens, tok_other, dq_keep, dq_got], us=5.0)
    early = ring_start(early, "x")
    keep3, send3 = run(back_x, [shape(64, width, F32), part64], [own, c1, c2, c3], [pltpu.VMEM((128, width), F32)])
    got3 = swap(send3, "core", 1)
    att_ring = ring_go_on(run.hold(*att_ring), "head")
    dkv_mine, dkv_their, dkv_keep, dkv_give = run(back_last, [square] * 4, [keep3, got3, got, dkv_local])
    dkv_got = swap(dkv_give, "core", 1)
    late = run(late_terms, ring_shapes(4, width, 128), [tokens, tok_other, dkv_keep, dkv_got], us=3.0)
    late = ring_start(late, "z")
    early = ring_go_on(ring_mid(run, early), "x")
    in_ring = run(input_parts, ring_shapes(rows, width),
                  [dq, dkv_mine, dkv_their, w1, w1_other, w2, w2_other], us=5.0)
    late = ring_go_on(ring_mid(run, late), "z")
    attended = run(ring_end, [square], att_ring)[0]
    in_ring = ring_start(run.hold(*in_ring), "head")
    early = send_parts(run(early_turn, part_shapes(width, 128), early), "z")
    in_ring = ring_go_on(ring_mid(run, in_ring), "head")
    late = send_parts(run(late_turn, part_shapes(width, 128), late), "x")
    grad_tokens = run(ring_end, [square], in_ring)[0]
    keep, give = run(chip_sums, [shape(64, 2 * width, F32)] * 2, [*early, *late], [pltpu.VMEM((128, 2 * width), F32)])
    grad_w_out, grad_w_query, grad_w_key, grad_w_value = run(
        last_parts, [shape(64, width, F32)] * 4, [keep, swap(give, "core", 1)])
    return (attended, grad_tokens, grad_w_query, grad_w_key, grad_w_value, grad_w_out.T)


def solution(mesh):
    fine = Mesh(mesh.devices.reshape(4, 4, 2, 4), SEQ + ("head",))
    in_specs = (
        P(SEQ, None),
        P(SEQ, None),
        P(None, "head"),
        P(None, "head"),
        P(None, "head"),
        P("head", None),
        P(),
    )
    out_specs = (P(SEQ, "head"),) * 5 + (P("head", SEQ),)
    return jax.shard_map(body, mesh=fine, in_specs=in_specs, out_specs=out_specs, check_vma=False)
```

```python
import math

import jax
import jax.numpy as jnp
from jax import lax
from jax.experimental import pallas as pl
from jax.experimental.pallas import tpu as pltpu
from jax.sharding import Mesh, PartitionSpec as P

DH = 128
LEAF = 128
PRIME = 32749
CAP = 6.0
HALF_NOISE = 0.5
SCALE = 1.0 / math.sqrt(DH)
BF = jnp.bfloat16
F32 = jnp.float32
SEQ = ("z", "x", "core")
VMEM = pl.BlockSpec(memory_space=pltpu.VMEM)
SMEM = pl.BlockSpec(memory_space=pltpu.SMEM)
HBM = pl.BlockSpec(memory_space=pltpu.HBM)
ANY = pl.BlockSpec(memory_space=pl.ANY)


def params(mib=24):
    return pltpu.CompilerParams(vmem_limit_bytes=mib << 20)


class Chain:
    def __init__(self):
        self.tick = None

    def call(self, kernel, outs, args, specs, scratch, us, mib=24, aliases={}, out_specs=None):
        first, used = self.tick is None, len(args)

        def run(*refs):
            ins, tick_in, rest = refs[:used], refs[used : used + 1 - first], refs[used + 1 - first :]
            rest[0][...] = jnp.zeros((1, 128), F32) if first else tick_in[0][...]
            kernel(here(), *ins, *rest[1:])

        ticks = [] if first else [self.tick]
        self.tick, *results = pl.pallas_call(
            run,
            out_shape=[shape(1, 128, F32), *outs],
            in_specs=specs + [VMEM] * len(ticks),
            out_specs=[VMEM] + (out_specs or [ANY if n in aliases else VMEM for n in range(len(outs))]),
            scratch_shapes=list(scratch),
            name=kernel.__name__,
            input_output_aliases={n: 1 + n for n in aliases},
            cost_estimate=pl.CostEstimate(flops=int(us * 2.5e9), bytes_accessed=1, transcendentals=0),
            compiler_params=params(mib),
        )(*args, *ticks)
        return results

    def __call__(self, kernel, outs, args, scratch=(), us=1.0):
        return self.call(kernel, outs, args, [VMEM] * len(args), scratch, us)

    def hold(self, *arrays):
        return self.call(
            wait_here, [jax.ShapeDtypeStruct(a.shape, a.dtype) for a in arrays], arrays, [ANY] * len(arrays), (), 0.1,
            aliases=range(len(arrays)))


def wait_here(place, *refs):
    pass


def here():
    return [lax.axis_index(name) for name in ("core", "x", "z", "head")]


def shape(rows, cols, dtype):
    return jax.ShapeDtypeStruct((rows, cols), dtype)


def dot(a, b):
    return jnp.dot(a, b, preferred_element_type=F32)


def dot_bt(a, b):
    return lax.dot_general(a, b, (((1,), (1,)), ((), ())), preferred_element_type=F32)


def dot_at(a, b):
    return lax.dot_general(a, b, (((0,), (0,)), ((), ())), preferred_element_type=F32)


def rows_at(start, count):
    return pl.ds(pl.multiple_of(start, count), count)


def halve(rows_in):
    rows = rows_in.shape[0]
    out_row = lax.broadcasted_iota(jnp.int32, (rows // 2, rows), 0)
    in_row = lax.broadcasted_iota(jnp.int32, (rows // 2, rows), 1)
    average = jnp.where(lax.shift_right_logical(in_row, 1) == out_row, 0.5, 0.0).astype(BF)
    return dot(average, rows_in).astype(BF)


def expand(rows_in, shift=1):
    rows, times = rows_in.shape[0], 1 << shift
    out_row = lax.broadcasted_iota(jnp.int32, (rows * times, rows), 0)
    in_row = lax.broadcasted_iota(jnp.int32, (rows * times, rows), 1)
    spread = jnp.where(lax.shift_right_logical(out_row, shift) == in_row, 1.0 / times, 0.0).astype(BF)
    high = rows_in.astype(BF)
    low = (rows_in - high.astype(F32)).astype(BF)
    return dot(spread, high) + dot(spread, low)


def fold(value):
    for _ in range(2):
        value = lax.shift_right_logical(value, 15) * 19 + (value & 32767)
    return value


def below_prime(value):
    return jnp.where(value >= PRIME, value - PRIME, value)


def hash_of(row_part, col_part, row_ids, col_ids):
    h = row_part + col_part
    f = h.astype(F32)
    quotient = (f * (f * (1.0 / PRIME))).astype(jnp.int32)
    h = h * h - quotient * PRIME + col_ids
    return below_prime(fold(h * h + row_ids)).astype(F32)


def add_squares(w_ref, start, rows, acc):
    def add(i, acc):
        w = w_ref[rows_at(start + i * 64, 64), :].astype(F32)
        return acc + jnp.sum((w * w).reshape(8, 8, w.shape[1]), axis=0)

    return lax.fori_loop(0, rows // 64, add, acc)


def noise_all(w_ref, out_ref, squares, rank, seed, lanes_are_rows, written):
    rows, cols = w_ref.shape
    chunk = 64
    mult, lane_mult = (10007, 7919) if lanes_are_rows else (7919, 10007)
    own_ids = lax.broadcasted_iota(jnp.int32, (1, cols), 1) + rank * cols
    own_part = below_prime(below_prime(fold(own_ids * lane_mult)) + below_prime(fold(seed * 31337)))
    mean = jnp.sum(squares, axis=0, keepdims=True) * (1.0 / rows)
    amp = HALF_NOISE * jnp.sqrt(mean + 1e-06)
    slope = amp * (2.0 / (PRIME - 1))

    def step(i, carry):
        ids, part = carry
        for lane in range(cols // 128):
            here = slice(lane * 128, lane * 128 + 128)
            lane_ids, lane_part = own_ids[:, here], own_part[:, here]
            if lanes_are_rows:
                hashed = hash_of(lane_part, part, lane_ids, ids)
            else:
                hashed = hash_of(part, lane_part, ids, lane_ids)
            w = w_ref[rows_at(i * chunk, chunk), here].astype(F32)
            out_ref[rows_at(i * chunk, chunk), here] = ((w - amp[:, here]) + slope[:, here] * hashed).astype(BF)
        return ids + chunk, below_prime(part + chunk * mult % PRIME)

    ids = lax.broadcasted_iota(jnp.int32, (chunk, 128), 0)
    carry = (ids, ids * mult % PRIME)
    steps = rows // chunk // 4
    for n in range(4):
        carry = lax.fori_loop(n * steps, n * steps + steps, step, carry, unroll=2)
        written(n)


def perturb_one(w_from, x_from, seed, rank, out_hbm, own_ref, w_ref, x_ref, new_ref, sems, turned):
    rows, cols = new_ref.shape
    piece, quarter = w_ref.shape[0] // 8, rows // 4
    x_copy = pltpu.make_async_copy(x_from, x_ref, sems.at[8])
    ins = [
        pltpu.make_async_copy(w_from.at[pl.ds(n * piece, piece), :], w_ref.at[pl.ds(n * piece, piece), :], sems.at[n])
        for n in range(8)
    ]
    outs = [
        pltpu.make_async_copy(
            new_ref.at[pl.ds(n * quarter, quarter), :], out_hbm.at[pl.ds(n * quarter, quarter), :], sems.at[9 + n])
        for n in range(4)
    ]
    for copy in ins:
        copy.start()
    squares = jnp.zeros((8, cols), F32)
    for n, copy in enumerate(ins):
        copy.wait()
        if turned is None:
            squares = add_squares(w_ref, n * piece, piece, squares)
    x_copy.start()
    if turned is not None:
        for n in range(rows // 128):
            turned[n * 128 : n * 128 + 128, :] = w_ref[:, n * 128 : n * 128 + 128].T
        squares = add_squares(turned, 0, rows, squares)
        w_ref = turned
    noise_all(w_ref, new_ref, squares, rank, seed, turned is not None, lambda n: outs[n].start())
    x_copy.wait()
    for n in range(2):
        part = slice(n * x_ref.shape[0] // 2, (n + 1) * x_ref.shape[0] // 2)
        own_ref[part, :] = dot(x_ref[part, :], new_ref[...]).astype(BF)
    for copy in outs:
        copy.wait()


def perturb_same(place, seeds_ref, w0_ref, w1_ref, x_from, out_hbm, own_ref, w_ref, x_ref, new_ref, sems):
    for core, w_from in ((0, w0_ref), (1, w1_ref)):

        @pl.when(place[0] == core)
        def _(core=core, w_from=w_from):
            perturb_one(w_from, x_from, seeds_ref[1 + core], place[3], out_hbm, own_ref, w_ref, x_ref, new_ref, sems, None)


def perturb_mixed(place, seeds_ref, w0_ref, w1_ref, x0_from, x1_from, out_hbm, own_ref, w_ref, x_ref, new_ref, sems, wide_ref):
    @pl.when(place[0] == 0)
    def _():
        perturb_one(w0_ref, x0_from, seeds_ref[0], place[3], out_hbm, own_ref, w_ref, x_ref, new_ref, sems, None)

    @pl.when(place[0] == 1)
    def _():
        perturb_one(w1_ref, x1_from, seeds_ref[3], place[3], out_hbm, own_ref, wide_ref, x_ref, new_ref, sems, w_ref)


def perturb(run, kernel, seeds, w0, w1, activations, mib):
    rows, cols = w0.shape
    tokens = activations[0].shape
    wide = [pltpu.VMEM(w1.shape, BF)] if w1.shape != w0.shape else []
    return run.call(
        kernel, [shape(rows, cols, BF), shape(tokens[0], cols, BF)], [seeds, w0, w1, *activations],
        [SMEM] + [HBM] * (2 + len(activations)),
        [pltpu.VMEM((rows, cols), BF), pltpu.VMEM(tokens, BF), pltpu.VMEM((rows, cols), BF), pltpu.SemaphoreType.DMA((13,))]
        + wide, 7.0, mib, out_specs=[HBM, VMEM])


def capped(k, q):
    t = jnp.tanh(dot_bt(k, q) * (SCALE / CAP))
    return t, jnp.exp(CAP * t)


def levels_kernel(place, own_ref, other_ref, send_ref, near_ref, chip_ref, chip_next_ref):
    core = place[0]
    send_ref[...] = halve(halve(own_ref[...]))
    near_ref[...] = halve(halve(other_ref[...]))
    chip_ref[rows_at(core * 64, 64), :] = halve(send_ref[...])
    chip_ref[rows_at(64 - core * 64, 64), :] = halve(near_ref[...])
    chip_next_ref[...] = halve(chip_ref[...])


def local_forward(place, mine_ref, their_ref, w2_mine_ref, w2_their_ref,
                  q_ref, ga_ref, kl_ref, vl_ref, num_ref, sum_ref):
    for core, (first, second, q_in, ga_in) in (
        (0, (kl_ref, vl_ref, w2_mine_ref, w2_their_ref)),
        (1, (vl_ref, kl_ref, w2_their_ref, w2_mine_ref)),
    ):

        @pl.when(place[0] == core)
        def _(first=first, second=second, q_in=q_in, ga_in=ga_in):
            q_ref[...] = q_in[...]
            ga_ref[...] = ga_in[...]
            for into, rows_in in ((first, mine_ref), (second, their_ref)):
                upper = halve(rows_in[...])
                into[:256, :] = rows_in[:256, :]
                into[256:384, :] = upper[128:, :]
                into[384:640, :] = rows_in[256:, :]
                into[640:, :] = upper[:128, :]

    for h in range(q_ref.shape[1] // DH):
        hs = slice(h * DH, h * DH + DH)
        for pair in range(2):
            rows, keys = slice(pair * 256, pair * 256 + 256), slice(pair * 384, pair * 384 + 384)
            _, e = capped(kl_ref[keys, hs], q_ref[rows, hs])
            w = jnp.concatenate([e[:256], 2.0 * e[256:]], axis=0)
            num_ref[hs, rows] = dot_at(vl_ref[keys, hs], w.astype(BF))
            sum_ref[h : h + 1, rows] = jnp.sum(w, axis=0, keepdims=True)


def far_kernel(place, q_ref, near_mine, near_their, mine_a, mine_b, their_a, their_b, num_ref, sum_ref, ga_ref,
               att_ref, att_keep, att_give, inv_ref, rd_ref, dq_ref, keep_ref, send_ref, kf, vf, dkf, dvf):
    core = place[0]
    for is_core, (mine, their) in ((0, (kf, vf)), (1, (vf, kf))):

        @pl.when(core == is_core)
        def _(mine=mine, their=their):
            for into, near, first, second in ((mine, near_mine, mine_a, mine_b), (their, near_their, their_a, their_b)):
                into[:128, :] = near[...]
                into[128:384, :] = first[...]
                into[384:, :] = second[...]

    for h in range(q_ref.shape[1] // DH):
        hs = slice(h * DH, h * DH + DH)
        q, k, v, ga = q_ref[:, hs], kf[:, hs], vf[:, hs], ga_ref[:, hs]
        t, e = capped(k, q)
        w = jnp.concatenate([e[n * 128 : n * 128 + 128] * float(4 << n) for n in range(5)], axis=0)
        inv = 1.0 / (sum_ref[h : h + 1, :] + jnp.sum(w, axis=0, keepdims=True))
        att = ((num_ref[hs, :] + dot_at(v, w.astype(BF))) * inv).T.astype(BF)
        att_ref[:, hs] = att
        rd = jnp.sum((ga.astype(F32) * att.astype(F32)).T, axis=0, keepdims=True)
        inv_ref[h : h + 1, :] = inv
        rd_ref[h : h + 1, :] = rd
        p = w * inv
        dvf[:, hs] = dot(p.astype(BF), ga)
        g = (p * (dot_bt(v, ga) - rd) * (1.0 - t * t)).astype(BF)
        dq_ref[hs, :] = dot_at(k, g)
        dkf[:, hs] = dot(g, q) * SCALE

    half = att_keep.shape[1]
    att_keep[...] = att_ref[:, rows_at(core * half, half)]
    att_give[...] = att_ref[:, rows_at(half - core * half, half)]
    send_ref[:128, :] = dkf[:128, :].astype(BF)
    send_ref[128:256, :] = dvf[:128, :].astype(BF)
    for is_core, (keep, give) in ((0, (dkf, dvf)), (1, (dvf, dkf))):

        @pl.when(core == is_core)
        def _(keep=keep, give=give):
            keep_ref[...] = keep[128:, :]
            send_ref[256:, :] = give[128:, :].astype(BF)


def local_backward(place, q_ref, kl_ref, vl_ref, inv_ref, rd_ref, ga_ref, dqf_ref,
                   dq_ref, dq_keep, dq_give, dkv_ref, d1_ref):
    width = q_ref.shape[1]
    for h in range(width // DH):
        hs = slice(h * DH, h * DH + DH)
        hv = slice(width + h * DH, width + h * DH + DH)
        for pair in range(2):
            rows, keys = slice(pair * 256, pair * 256 + 256), slice(pair * 384, pair * 384 + 384)
            other = slice((1 - pair) * 128, (1 - pair) * 128 + 128)
            q, ga, k, v = q_ref[rows, hs], ga_ref[rows, hs], kl_ref[keys, hs], vl_ref[keys, hs]
            t, e = capped(k, q)
            inv = inv_ref[h : h + 1, rows]
            p = jnp.concatenate([e[:256] * inv, e[256:] * (2.0 * inv)], axis=0)
            dv = dot(p.astype(BF), ga)
            g = (p * (dot_bt(v, ga) - rd_ref[h : h + 1, rows]) * (1.0 - t * t)).astype(BF)
            dq_ref[rows, hs] = ((dqf_ref[hs, rows] + dot_at(k, g)) * SCALE).T.astype(BF)
            dk = dot(g, q) * SCALE
            dkv_ref[rows, hs] = dk[:256]
            dkv_ref[rows, hv] = dv[:256]
            d1_ref[other, hs] = dk[256:]
            d1_ref[other, hv] = dv[256:]
    dkv_ref[...] += expand(d1_ref[...])
    core, half = place[0], dq_keep.shape[1]
    dq_keep[...] = dq_ref[:, rows_at(core * half, half)]
    dq_give[...] = dq_ref[:, rows_at(half - core * half, half)]


def out_x(place, own_ref, one_ref, two_ref, three_ref, sets_ref, row_ref, row_next_ref):
    x = place[1]
    odd = x & 1
    sets_ref[:128, :] = one_ref[...]
    sets_ref[rows_at(128 + 64 * odd, 64), :] = two_ref[...]
    sets_ref[rows_at(192 - 64 * odd, 64), :] = three_ref[...]
    for apart, part in ((0, own_ref[...]), (1, halve(one_ref[...])), (2, two_ref[...]), (3, three_ref[...])):
        row_ref[rows_at(32 * (x ^ apart), 32), :] = halve(part)
    row_next_ref[...] = halve(row_ref[...])


def out_z(place, one_ref, two_ref, three_ref, sets_ref):
    odd = place[2] & 1
    sets_ref[:128, :] = one_ref[...]
    sets_ref[rows_at(128 + 64 * odd, 64), :] = two_ref[...]
    sets_ref[rows_at(192 - 64 * odd, 64), :] = three_ref[...]


def back_core(place, keep_ref, got_ref, near_ref, one_ref, two_ref, three_ref):
    odd = place[2] & 1
    near_ref[...] = keep_ref[:256, :] + got_ref[256:512, :].astype(F32)
    one_ref[...] = (keep_ref[256:384, :] + got_ref[512:640, :].astype(F32)).astype(BF)
    for into, first in ((two_ref, odd), (three_ref, 1 - odd)):
        kept = keep_ref[rows_at(384 + 64 * first, 64), :]
        into[...] = (kept + got_ref[rows_at(640 + 64 * first, 64), :].astype(F32)).astype(BF)


def back_z(place, near_ref, one_ref, two_ref, three_ref, own_out, one_out, two_out, three_out, row_ref):
    x = place[1]
    odd = x & 1
    row_ref[...] = one_ref[...].astype(F32) + expand(two_ref[...].astype(F32) + three_ref[...].astype(F32))

    def part(apart):
        return row_ref[rows_at(32 * (x ^ apart), 32), :]

    own_out[...] = part(0)
    one_out[...] = (near_ref[:128, :] + expand(part(1), 2)).astype(BF)
    for into, apart, first in ((two_out, 2, odd), (three_out, 3, 1 - odd)):
        into[...] = (near_ref[rows_at(128 + 64 * first, 64), :] + expand(part(apart))).astype(BF)


def back_x(place, own_ref, one_ref, two_ref, three_ref, keep_ref, send_ref, chip_ref):
    core = place[0]
    pair = two_ref[...].astype(F32) + three_ref[...].astype(F32) + expand(own_ref[...])
    chip_ref[...] = one_ref[...].astype(F32) + expand(pair)
    keep_ref[...] = chip_ref[rows_at(64 * core, 64), :]
    send_ref[...] = chip_ref[rows_at(64 - 64 * core, 64), :].astype(BF)


def back_last(place, keep3_ref, got3_ref, got_ref, dkv_ref, mine_ref, their_ref, keep_ref, give_ref):
    width = keep3_ref.shape[1]
    half = width // 2
    for core in range(2):

        @pl.when(place[0] == core)
        def _(core=core):
            for n in range(2):
                upper = keep3_ref[...] if n == core else got3_ref[...].astype(F32)
                level = got_ref[n * 128 : n * 128 + 128, :].astype(F32) + expand(upper)
                done = (dkv_ref[:, n * width : n * width + width] + expand(level, 2)).astype(BF)
                (mine_ref if n == core else their_ref)[...] = done
                keep_ref[:, n * half : n * half + half] = done[:, core * half : core * half + half]
                give_ref[:, n * half : n * half + half] = done[:, half - core * half : width - core * half]


def part_shapes(*dims):
    return [jax.ShapeDtypeStruct(dims, F32)] + [jax.ShapeDtypeStruct(dims, BF)] * 3


def send_parts(parts, axis):
    own, one, two, three = parts
    return own, shift(one, axis, 1), shift(two, axis, 2), shift(three, axis, -1)


def total(own, one, two, three):
    return own + one.astype(F32) + two.astype(F32) + three.astype(F32)


def ring_shapes(*dims):
    half = (*dims[:-2], dims[-2] // 2, dims[-1])
    full = [jax.ShapeDtypeStruct(dims, BF)] * 2
    return [jax.ShapeDtypeStruct(half, BF)] * 2 + full + [jax.ShapeDtypeStruct(dims, F32)]


def ring_start(parts, axis):
    two_up, two_down, one, three, own = parts
    return shift(two_up, axis, 1), shift(two_down, axis, -1), one, three, own


def ring_middle(place, one_ref, three_ref, up_ref, down_ref, up_out, down_out):
    half = up_ref.shape[-2]
    low, high = (..., slice(0, half), slice(None)), (..., slice(half, None), slice(None))
    up_out[low] = (one_ref[low].astype(F32) + up_ref[...].astype(F32)).astype(BF)
    up_out[high] = one_ref[high]
    down_out[low] = three_ref[low]
    down_out[high] = (three_ref[high].astype(F32) + down_ref[...].astype(F32)).astype(BF)


def ring_mid(run, ring):
    up, down, one, three, own = ring
    return *run(ring_middle, [jax.ShapeDtypeStruct(one.shape, BF)] * 2, [one, three, up, down]), own


def ring_go_on(ring, axis):
    up, down, own = ring
    return own, shift(up, axis, 1), shift(down, axis, -1)


def ring_total(own, up, down):
    return own + up.astype(F32) + down.astype(F32)


def ring_end(place, own_ref, up_ref, down_ref, out_ref):
    out_ref[...] = ring_total(own_ref[...], up_ref[...], down_ref[...]).astype(BF)


def ring_parts(rank, outs):
    return ((rank + 2) & 3, None), ((rank + 1) & 3, outs[2]), ((rank + 3) & 3, outs[3]), (rank, outs[4])


def write_ring(rank, width, product, outs):
    for whose, into in ring_parts(rank, outs):
        part = product(rows_at(whose * width, width))
        if into is None:
            rows = part.shape[0] // 2
            outs[0][...] = part[:rows].astype(BF)
            outs[1][...] = part[rows:].astype(BF)
        else:
            into[...] = part.astype(into.dtype)


def attended_parts(place, att_ref, w2_mine, w2_their, *outs):
    for core, w_ref in ((0, w2_their), (1, w2_mine)):

        @pl.when(place[0] == core)
        def _(w_ref=w_ref):
            write_ring(place[3], att_ref.shape[1], lambda rows: dot_bt(att_ref[...], w_ref[rows, :]), outs)


def input_parts(place, dq_ref, mine_ref, their_ref, w1_mine, w1_their, w2_mine, w2_their, *outs):
    for core, wq_ref in ((0, w2_mine), (1, w2_their)):

        @pl.when(place[0] == core)
        def _(wq_ref=wq_ref):
            def product(rows):
                terms = dot_bt(dq_ref[...], wq_ref[rows, :]) + dot_bt(mine_ref[...], w1_mine[rows, :])
                return terms + dot_bt(their_ref[...], w1_their[rows, :])

            write_ring(place[3], dq_ref.shape[1], product, outs)


def gradient_blocks(lhs, lhs_other, keep, got, cols):
    grads = jnp.concatenate([keep[...].T, got[...].T], axis=1)
    rows = [jnp.concatenate([lhs[:, c], lhs_other[:, c]], axis=0) for c in cols]
    return dot(grads, jnp.concatenate(rows, axis=1))


def early_terms(place, cot, cot_other, att_keep, att_got, tok, tok_other, dq_keep, dq_got, *outs):
    half = att_keep.shape[1]
    for n, sources in enumerate(((cot, cot_other, att_keep, att_got), (tok, tok_other, dq_keep, dq_got))):
        for whose, into in ring_parts(place[1], outs):
            at = n * half
            if into is None:
                into, at = outs[n], 0
            for pair in range(2):
                cols = [rows_at((2 * pair + m) * 512 + whose * 128, 128) for m in range(2)]
                part = gradient_blocks(*sources, cols).astype(into.dtype)
                for m in range(2):
                    into[2 * pair + m, at : at + half, :] = part[:, m * 128 : m * 128 + 128]


def late_terms(place, tok, tok_other, keep, got, *outs):
    half = outs[0].shape[1]
    for whose, into in ring_parts(place[2], outs):
        for pair in range(2):
            part = gradient_blocks(tok, tok_other, keep, got, [rows_at(whose * 512 + pair * 256, 256)])
            for n in range(2):
                block = part[:, n * 128 : n * 128 + 128]
                if into is None:
                    outs[0][2 * pair + n] = block[:half].astype(BF)
                    outs[1][2 * pair + n] = block[half:].astype(BF)
                else:
                    into[2 * pair + n] = block.astype(into.dtype)


def early_turn(place, *refs):
    turn(place[2], *refs)


def late_turn(place, *refs):
    turn(place[1], *refs)


def turn(at, own_ref, up_ref, down_ref, *outs):
    for by, into in enumerate(outs):
        n = (at + by) & 3
        into[...] = ring_total(own_ref[n], up_ref[n], down_ref[n]).astype(into.dtype)


def chip_sums(place, *refs):
    early, late, (keep_ref, give_ref, turned) = refs[:4], refs[4:8], refs[8:]
    width = early[0].shape[0]
    for n, parts in enumerate((early, late)):
        turned[:, n * width : n * width + width] = total(*(r[...] for r in parts)).T
    keep_ref[...] = turned[rows_at(place[0] * 64, 64), :]
    give_ref[...] = turned[rows_at(64 - place[0] * 64, 64), :]


def last_parts(place, keep_ref, got_ref, *outs):
    half = outs[0].shape[1] // 2
    for core in range(2):

        @pl.when(place[0] == core)
        def _(core=core):
            for from_ref, side in ((keep_ref, core), (got_ref, 1 - core)):
                for n, into in enumerate(outs):
                    into[:, side * half : side * half + half] = from_ref[:, n * half : n * half + half]


def swap(rows, axis, apart):
    return lax.ppermute(rows, axis, [(i, i ^ apart) for i in range(lax.axis_size(axis))])


def shift(rows, axis, by):
    n = lax.axis_size(axis)
    return lax.ppermute(rows, axis, [(i, (i + by) % n) for i in range(n)])


def body(tokens, cotangent, w_query, w_key, w_value, w_out, seeds):
    run = Chain()
    core = lax.axis_index("core")
    rows = tokens.shape[0]
    width = w_query.shape[1]
    square, stats = shape(rows, width, BF), shape(width // DH, rows, F32)
    half_cols, turned = shape(rows, width // 2, BF), shape(width, rows, F32)
    part128, part64 = shape(128, width, BF), shape(64, width, BF)

    tok_other, cot_other = swap(tokens, "core", 1), swap(cotangent, "core", 1)

    w1, mine0 = perturb(run, perturb_same, seeds, w_key, w_value, [tokens], 56)
    give0 = dot(tok_other, w1).astype(BF)
    their0 = swap(give0, "core", 1)
    w1_other = swap(w1, "core", 1)
    cot_other = run.hold(cot_other)[0]
    level2, near_mine, chip, chip_next = run(levels_kernel, [part128] * 3 + [part64], [mine0, give0])
    x1, x2, x3 = swap(chip, "x", 1), swap(chip_next, "x", 2), swap(chip_next, "x", 3)
    near_their = swap(level2, "core", 1)
    their0, near_their, w1_other = run.hold(their0, near_their, w1_other)

    w2, mine2 = perturb(run, perturb_mixed, seeds, w_query, w_out, [tokens, cotangent], 56)
    mine_a, row, row_next = run(out_x, [shape(256, width, BF), part128, part64], [chip_next, x1, x2, x3])
    z1, z2, z3 = swap(row, "z", 1), swap(row_next, "z", 2), swap(row_next, "z", 3)
    their_a = swap(mine_a, "core", 1)
    w2 = run.hold(w2)[0]
    give2 = dot(jnp.where(core == 0, tok_other, cot_other), w2).astype(BF)
    their2 = swap(give2, "core", 1)
    their_a, their2, w2 = run.hold(their_a, their2, w2)
    w2_other = swap(w2, "core", 1)

    queries, grad_att, kl, vl, num, total = run(
        local_forward, [square] * 2 + [shape(768, width, BF)] * 2 + [turned, stats], [mine0, their0, mine2, their2], us=3.0)
    mine_b = run(out_z, [shape(256, width, BF)], [z1, z2, z3])[0]
    their_b = swap(mine_b, "core", 1)
    att, att_keep, att_give, inv, rd, dq_far, keep, send = run(
        far_kernel,
        [square] + [half_cols] * 2 + [stats] * 2 + [turned, shape(512, width, F32), shape(768, width, BF)],
        [queries, near_mine, near_their, mine_a, mine_b, their_a, their_b, num, total, grad_att],
        [pltpu.VMEM((640, width), BF)] * 2 + [pltpu.VMEM((640, width), F32)] * 2, us=6.0)
    got, att_got = swap(send, "core", 1), swap(att_give, "core", 1)

    att_ring = run(attended_parts, ring_shapes(rows, width), [att, w2, w2_other], us=2.0)
    got, att_got = run.hold(got, att_got)
    near, b1, b2, b3 = run(back_core, [shape(256, width, F32), part128, part64, part64], [keep, got])
    b1, b2, b3 = swap(b1, "z", 1), swap(b2, "z", 2), swap(b3, "z", 3)
    att_ring = ring_start(att_ring, "head")
    dq, dq_keep, dq_give, dkv_local = run(
        local_backward, [square, half_cols, half_cols, shape(rows, 2 * width, F32)],
        [queries, kl, vl, inv, rd, grad_att, dq_far], [pltpu.VMEM((256, 2 * width), F32)], us=4.0)
    own, c1, c2, c3 = run(
        back_z, [shape(32, width, F32), part128, part64, part64], [near, b1, b2, b3], [pltpu.VMEM((128, width), F32)])
    c1, c2, c3 = swap(c1, "x", 1), swap(c2, "x", 2), swap(c3, "x", 3)
    dq_give = run.hold(dq_give)[0]
    dq_got = swap(dq_give, "core", 1)
    att_ring = ring_mid(run, att_ring)
    early = run(
        early_terms, ring_shapes(4, width, 128),
        [cotangent, cot_other, att_keep, att_got, tokens, tok_other, dq_keep, dq_got], us=5.0)
    early = ring_start(early, "x")
    keep3, send3 = run(back_x, [shape(64, width, F32), part64], [own, c1, c2, c3], [pltpu.VMEM((128, width), F32)])
    got3 = swap(send3, "core", 1)
    att_ring = ring_go_on(run.hold(*att_ring), "head")
    dkv_mine, dkv_their, dkv_keep, dkv_give = run(back_last, [square] * 4, [keep3, got3, got, dkv_local])
    dkv_got = swap(dkv_give, "core", 1)
    late = run(late_terms, ring_shapes(4, width, 128), [tokens, tok_other, dkv_keep, dkv_got], us=3.0)
    late = ring_start(late, "z")
    early = ring_go_on(ring_mid(run, early), "x")
    in_ring = run(input_parts, ring_shapes(rows, width),
                  [dq, dkv_mine, dkv_their, w1, w1_other, w2, w2_other], us=5.0)
    late = ring_go_on(ring_mid(run, late), "z")
    attended = run(ring_end, [square], att_ring)[0]
    in_ring = ring_start(run.hold(*in_ring), "head")
    early = send_parts(run(early_turn, part_shapes(width, 128), early), "z")
    in_ring = ring_go_on(ring_mid(run, in_ring), "head")
    late = send_parts(run(late_turn, part_shapes(width, 128), late), "x")
    grad_tokens = run(ring_end, [square], in_ring)[0]
    keep, give = run(chip_sums, [shape(64, 2 * width, F32)] * 2, [*early, *late], [pltpu.VMEM((128, 2 * width), F32)])
    grad_w_out, grad_w_query, grad_w_key, grad_w_value = run(
        last_parts, [shape(64, width, F32)] * 4, [keep, swap(give, "core", 1)])
    return (attended, grad_tokens, grad_w_query, grad_w_key, grad_w_value, grad_w_out.T)


def solution(mesh):
    fine = Mesh(mesh.devices.reshape(4, 4, 2, 4), SEQ + ("head",))
    in_specs = (
        P(SEQ, None),
        P(SEQ, None),
        P(None, "head"),
        P(None, "head"),
        P(None, "head"),
        P("head", None),
        P(),
    )
    out_specs = (P(SEQ, "head"),) * 5 + (P("head", SEQ),)
    return jax.shard_map(body, mesh=fine, in_specs=in_specs, out_specs=out_specs, check_vma=False)
```
